512 devices in a mesh: dp: 32 (over y_lo, z), fsdp: 16 (over x, y_hi, core).
Axes of the slice: x: 4, y: 4 (y_hi: 2, y_lo: 2; y = y_hi * 2 + y_lo), z: 16, core: 2. Of those that a mesh axis runs over, the one named last changes fastest.
Arguments:
- train_layer_inputs: bfloat16 [320, 96, 8192], P('dp', None, 'fsdp'), may hold values from -6 to 6
- train_output_gradients: bfloat16 [320, 96, 8192], P('dp', None, 'fsdp'), may hold values from -6 to 6
- train_target_tokens: int32 [320, 96], P('dp'), may hold values from -100 to 128255, as said below
- validation_layer_inputs: bfloat16 [256, 96, 8192], P('dp', None, 'fsdp'), may hold values from -6 to 6
- validation_output_gradients: bfloat16 [256, 96, 8192], P('dp', None, 'fsdp'), may hold values from -6 to 6
- validation_target_tokens: int32 [256, 96], P('dp'), may hold values from -100 to 128255, as said below
- adapter_down: bfloat16 [64, 8192], P(None, 'fsdp'), may hold values from -0.0625 to 0.0625
- adapter_up: bfloat16 [64, 8192], P(None, 'fsdp'), may hold values from -0.0625 to 0.0625
- adam_first_moments: float32 [2, 64, 8192], P(None, None, 'fsdp'), may hold values from -0.4375 to 0.4375
- adam_second_moments: float32 [2, 64, 8192], P(None, None, 'fsdp'), may hold values from 0.0001 to 0.01
- rank_projection: bfloat16 [2, 64, 16], replicated, may hold values from -0.75 to 0.75
- feature_projection: bfloat16 [2, 8192, 256], P(None, 'fsdp')
Outputs:
- cosine: float32 [320, 256], P('dp', 'fsdp')
The draws below stay inside these ranges and needn't reach their ends.
Inputs may be any that keep to these rules, and one draw needn't show every extreme that they name: `train_target_tokens`: each segment begins with one or more positions labelled -100; at least its last 24 positions hold token ids below 128256. `validation_target_tokens`: each segment begins with one or more positions labelled -100; at least its last 24 positions hold token ids below 128256.
All inputs are finite; a program needn't handle non-finite values.
Results may differ from the reference program's by a relative error of at most 0.0055.
Values sent between devices are 32-bit elements; how exact they have to be, the bound alone decides.
A program may use at most 64 MiB of HBM per device.

```python
import math
from functools import partial
import jax
import jax.numpy as jnp
from jax import lax

MODEL_WIDTH = 8192
VOCAB = 128256
ADAPTER_RANK = 64
LEFT_DIM = 16
RIGHT_DIM = 256
SEG = 96
TRAIN_DEV = 10
VALID_DEV = 8
TRAIN_ALL = 320
VALID_ALL = 256
N_DP = 32
N_FSDP = 16


def segment_labels(key, count):
    first_key, second_key = jax.random.split(key)
    prompt = jax.random.randint(first_key, (count, 1), 1, 3 * SEG // 4 + 1)
    token_ids = jax.random.randint(second_key, (count, SEG), 0, VOCAB)
    token_ids = token_ids.at[0, SEG - 1].set(VOCAB - 1)
    position = jnp.arange(SEG)[None, :]
    return jnp.where(position < prompt, -100, token_ids).astype(jnp.int32)


def draw_train_target_tokens(key, part):
    key = jax.random.fold_in(key, 11)
    return segment_labels(key, TRAIN_DEV * N_DP)


def draw_validation_target_tokens(key, part):
    key = jax.random.fold_in(key, 13)
    return segment_labels(key, VALID_DEV * N_DP)


def draw_feature_projection(key, part):
    key = jax.random.fold_in(key, 17)
    base_key, pair_key = jax.random.split(key)
    base = jnp.clip(jax.random.normal(base_key, (2, MODEL_WIDTH, RIGHT_DIM), jnp.float32), -6.0, 6.0)
    growth = 10.0
    column = jnp.arange(RIGHT_DIM).astype(jnp.float32) / RIGHT_DIM
    column_scale = growth ** column
    pairing = jax.random.permutation(pair_key, N_FSDP)
    row_block = jnp.arange(MODEL_WIDTH) // (MODEL_WIDTH // N_FSDP)
    column_block = jnp.arange(RIGHT_DIM) // (RIGHT_DIM // N_FSDP)
    spiked = jnp.where(pairing[row_block][:, None] == column_block[None, :], 3.0, 1.0)
    return (base * column_scale[None, None, :] * spiked[None, :, :] / jnp.sqrt(float(MODEL_WIDTH))).astype(jnp.bfloat16)


def level_of(rng, dims, cuts, smallest, top_value):
    gain = 1.0
    for axis_at, blocks in cuts:
        heights = jax.random.uniform(jax.random.fold_in(jax.random.fold_in(rng, 6), axis_at), (blocks,), jnp.float32, smallest / len(cuts), top_value / len(cuts))
        gain = gain * jnp.repeat(jnp.exp(heights), dims[axis_at] // blocks).reshape((-1,) + (1,) * (len(dims) - 1 - axis_at))
    return gain


def scatter_about(own_key, shape, scale, limit, shards=(), dtype=jnp.bfloat16):
    gain = level_of(own_key, shape, shards, -0.22, 0.18) if shards else 1.0
    values = jax.random.normal(own_key, shape, jnp.float32) * scale * gain
    return jnp.minimum(jnp.maximum(values, -limit), limit).astype(dtype)


def setup_inputs(seed: int = 0) -> dict:
    seeds = jax.random.split(jax.random.key(seed), 13)
    return {
        "train_layer_inputs": scatter_about(seeds[0], (TRAIN_ALL, SEG, MODEL_WIDTH), 1.0, 6.0, ((0, 32), (2, 16))),
        "train_output_gradients": scatter_about(seeds[1], (TRAIN_ALL, SEG, MODEL_WIDTH), 1.0, 6.0, ((0, 32), (2, 16))),
        "train_target_tokens": draw_train_target_tokens(jax.random.fold_in(seeds[12], 71), 0),
        "validation_layer_inputs": scatter_about(seeds[3], (VALID_ALL, SEG, MODEL_WIDTH), 1.0, 6.0, ((0, 32), (2, 16))),
        "validation_output_gradients": scatter_about(seeds[4], (VALID_ALL, SEG, MODEL_WIDTH), 1.0, 6.0, ((0, 32), (2, 16))),
        "validation_target_tokens": draw_validation_target_tokens(jax.random.fold_in(seeds[12], 71), 0),
        "adapter_down": scatter_about(seeds[6], (ADAPTER_RANK, MODEL_WIDTH), MODEL_WIDTH ** -0.5, 0.0625, ((1, 16),)),
        "adapter_up": scatter_about(seeds[7], (ADAPTER_RANK, MODEL_WIDTH), MODEL_WIDTH ** -0.5, 0.0625, ((1, 16),)),
        "adam_first_moments": scatter_about(seeds[8], (2, ADAPTER_RANK, MODEL_WIDTH), 0.03, 0.4375, ((2, 16),), jnp.float32),
        "adam_second_moments": jnp.clip(jnp.exp(math.log(0.01) - 4.6051702 * jax.random.uniform(seeds[9], (2, ADAPTER_RANK, MODEL_WIDTH), jnp.float32) ** level_of(seeds[9], (2, ADAPTER_RANK, MODEL_WIDTH), ((2, 16),), -0.2, 0.2)), 0.0001, 0.01),
        "rank_projection": scatter_about(seeds[10], (2, ADAPTER_RANK, LEFT_DIM), ADAPTER_RANK ** -0.5, 0.75),
        "feature_projection": draw_feature_projection(jax.random.fold_in(seeds[12], 71), 0),
    }


ADAPTER_SCALE = 2.0
BETA_FIRST = 0.9
BETA_SECOND = 0.999
ADAM_EPS = 1e-08
NORM_EPS = 1e-06

def segment_feature_rows(adapter_down, adapter_up, adam_first_moments, adam_second_moments, rank_projection, right_expanded, adapted_output, input_rows):
    layer_inputs, output_gradient, labels = input_rows
    down_inner_product = jnp.dot(layer_inputs, adapter_down.T, preferred_element_type=jnp.float32)
    up_inner_product = jnp.dot(output_gradient, adapter_up.T, preferred_element_type=jnp.float32)
    retained_mask = (labels != -100).astype(jnp.float32)
    if adapted_output:
        weight_values = retained_mask * (ADAPTER_SCALE / jnp.sum(retained_mask))
    else:
        weight_values = retained_mask
    scaled_up = (up_inner_product * weight_values[:, None]).astype(jnp.bfloat16)
    scaled_down = (down_inner_product * weight_values[:, None]).astype(jnp.bfloat16)
    grad_down = jnp.dot(scaled_up.T, layer_inputs, preferred_element_type=jnp.float32)
    grad_up = jnp.dot(scaled_down.T, output_gradient, preferred_element_type=jnp.float32)
    gradient = jnp.stack([grad_down, grad_up])
    if adapted_output:
        first_moment = BETA_FIRST * adam_first_moments + (1.0 - BETA_FIRST) * gradient
        second_moment = BETA_SECOND * adam_second_moments + (1.0 - BETA_SECOND) * gradient * gradient
        direction = (first_moment / (jnp.sqrt(second_moment) + ADAM_EPS)).astype(jnp.bfloat16)
    else:
        direction = gradient.astype(jnp.bfloat16)
    left_part = jnp.einsum('cia,cij->caj', rank_projection.astype(jnp.float32), direction.astype(jnp.float32), precision=lax.Precision.HIGHEST)
    return jnp.einsum('caj,cjb->cab', left_part, right_expanded, precision=lax.Precision.HIGHEST)

def unit_rows(features):
    flattened = features.reshape(features.shape[0], -1)
    return flattened / jnp.sqrt(lax.optimization_barrier(jnp.sum(flattened * flattened, axis=1, keepdims=True)) + NORM_EPS)

def reference(train_layer_inputs, train_output_gradients, train_target_tokens, validation_layer_inputs, validation_output_gradients, validation_target_tokens, adapter_down, adapter_up, adam_first_moments, adam_second_moments, rank_projection, feature_projection):
    right_expanded = feature_projection.astype(jnp.float32)
    train_function = partial(segment_feature_rows, adapter_down, adapter_up, adam_first_moments, adam_second_moments, rank_projection, right_expanded, True)
    validation_function = partial(segment_feature_rows, adapter_down, adapter_up, adam_first_moments, adam_second_moments, rank_projection, right_expanded, False)
    train_feats = lax.map(train_function, (train_layer_inputs, train_output_gradients, train_target_tokens))
    valid_feats = lax.map(validation_function, (validation_layer_inputs, validation_output_gradients, validation_target_tokens))
    return jnp.dot(unit_rows(train_feats), unit_rows(valid_feats).T, precision=lax.Precision.HIGHEST)
```

```python
import jax
import jax.numpy as jnp
from jax import lax
from jax.experimental import pallas as pl
from jax.experimental.pallas import tpu as pltpu
from jax.sharding import PartitionSpec as P

ADAPTER_SCALE = 2.0
BETA_FIRST = 0.9
BETA_SECOND = 0.999
ADAM_EPS = 1e-08
NORM_EPS = 1e-06

MESH = pl.DeviceIdType.MESH
F32 = jnp.float32
BF16 = jnp.bfloat16
SEG = 96
NT = 960
NV = 768
HALF = 512

OFFSETS = ((2, 1), (1, 1), (3, 1), (2, 0), (0, 1), (1, 0), (3, 0))
PAIR_OFFSETS = (4, 3, 5, 2, 6, 1, 7, 0)


def dot(a, b):
    return lax.dot_general(a, b, (((1,), (0,)), ((), ())), preferred_element_type=F32)


def dot_nt(a, b, precision=None):
    return lax.dot_general(
        a, b, (((1,), (1,)), ((), ())), preferred_element_type=F32, precision=precision
    )


def split(x):
    hi = x.astype(BF16)
    return hi, (x - hi.astype(F32)).astype(BF16)


def kernel(
    xt, ct, lt, xv, cv, lv, ad, au, mom1, mom2, rank_p, feat_p,
    out,
    buf, w, rp, fp, m_, v_, labt, labv,
    zp, ztw, ar, zf, wt, bd, pm8, pm2, dirs,
    pvl, pvtw, bvr, ptl, pttw, btr, vs, ts, vg, tg, ds, dr,
    ld, s_tw, r_tw, s_a1, r_a1, s_a2, r_a2, s_fw, r_fw, s_bv, r_bv, s_bt, r_bt,
    s_c, r_c, s_q, r_q, s_d, r_d, tok,
):
    d = lax.axis_index("dp")
    f = lax.axis_index("fsdp")
    y, z = lax.div(d, 16), lax.rem(d, 16)
    zm, zr = lax.div(z, 2), lax.rem(z, 2)
    q, k = lax.div(f, 2), lax.rem(f, 2)
    x, yh = lax.div(q, 2), lax.rem(q, 2)
    other = 1 - k
    twin = (d, f + 1 - 2 * k)
    chips = []
    for dx, dy in OFFSETS:
        to = lax.rem(x + dx, 4) * 2 + lax.rem(yh + dy, 2)
        fro = lax.rem(x + 4 - dx, 4) * 2 + lax.rem(yh + dy, 2)
        chips.append((to, fro))

    def dp_at(y_at, z_at):
        return y_at * 16 + z_at

    def z_off(n):
        return dp_at(y, lax.rem(z + n + 16, 16))

    loads = [
        (au, w.at[0]),
        (ad, w.at[1]),
        (rank_p, rp),
        (ct, buf.at[0, pl.ds(0, NT)]),
        (cv, buf.at[0, pl.ds(NT, NV)]),
        (xt, buf.at[1, pl.ds(0, NT)]),
        (xv, buf.at[1, pl.ds(NT, NV)]),
        (lt, labt),
        (lv, labv),
        (feat_p, fp),
        (mom1, m_),
        (mom2, v_),
    ]
    load = [pltpu.make_async_copy(a, b, ld.at[i]) for i, (a, b) in enumerate(loads)]
    for cp in load:
        cp.start()

    barrier = pltpu.get_barrier_semaphore()
    zt = z + 1 - 2 * zr
    greet = [(d, to * 2 + k) for to, _ in chips]
    greet += [twin, (dp_at(1 - y, z), f), (dp_at(y, zt), f), (dp_at(1 - y, zt), f)]
    greet += [(dp_at(y, lax.rem(z + 15 + 2 * zr, 16)), f)]
    for peer in greet:
        pl.semaphore_signal(barrier, inc=1, device_id=peer, device_id_type=MESH)

    def remote(src, dst, send, recv, peer):
        return pltpu.make_async_remote_copy(
            src_ref=src, dst_ref=dst, send_sem=send, recv_sem=recv,
            device_id=peer, device_id_type=MESH,
        )

    lane = lax.broadcasted_iota(jnp.int32, (16, 128), 1)

    def inner(c, at):
        wc = w[c]
        proj = lax.dot_general(
            rp[c], wc, (((0,), (0,)), ((), ())), preferred_element_type=F32
        )
        hi, lo = split(proj)
        both = jnp.concatenate([hi, lo], axis=0)
        for t in range(4):
            o = dot_nt(wc, buf[c, pl.ds(256 * t, 256), :])
            zp[at, :, 2 * t] = o[:, :128].reshape(8, 8, 128)
            if t < 3:
                zp[at, :, 2 * t + 1] = o[:, 128:].reshape(8, 8, 128)
            else:
                tail = o[:, 128:]
        for g in range(4):
            rows = jnp.concatenate(
                [
                    buf[c, pl.ds(NT + 192 * g, 128), :],
                    buf[c, pl.ds(NT + 192 * g + 64, 128), :],
                ],
                axis=0,
            )
            o = dot_nt(both, rows)
            o = o[:16] + o[16:]
            zp[at, 2 * g : 2 * g + 2, 8] = o[:, :128].reshape(2, 8, 128)
            mixed = jnp.where(lane < 64, tail[16 * g : 16 * g + 16], o[:, 128:])
            zp[at, 2 * g : 2 * g + 2, 7] = mixed.reshape(2, 8, 128)

    for i in range(7):
        load[i].wait()
    inner(other, 0)
    pl.semaphore_wait(barrier, len(greet))
    tw_a = remote(zp.at[0], ztw, s_tw.at[0], r_tw.at[0], twin)
    tw_a.start()
    for n in (-1, 1):
        pl.semaphore_signal(tok.at[0], inc=1, device_id=(z_off(n), f), device_id_type=MESH)
    inner(k, 1)
    tw_a.wait_recv()
    zp[1] = zp[1] + ztw[...]
    a1 = [
        remote(zp.at[1, to], ar.at[i], s_a1.at[i], r_a1.at[i], (d, to * 2 + k))
        for i, (to, _) in enumerate(chips)
    ]
    for cp in a1:
        cp.start()

    for i in range(7, 12):
        load[i].wait()
    iota = lambda shape, dim: lax.broadcasted_iota(jnp.int32, shape, dim)
    one = lambda cond: jnp.where(cond, 1.0, 0.0)
    tl = iota((1, 1024), 1)
    seg = jnp.zeros((1, 1024), jnp.int32)
    for j in range(1, 11):
        seg = seg + jnp.where(tl >= SEG * j, 1, 0)
    kept = one(labt[...] != -100)
    scale = ADAPTER_SCALE / jnp.sum(kept, axis=1, keepdims=True)
    spread = one(iota((SEG, 1024), 0) == tl - SEG * seg).astype(BF16)
    laid = dot(kept.astype(BF16), spread)
    wt[0:10, :] = jnp.where(iota((10, 1024), 0) == seg, laid * scale, 0.0)
    grp = lax.shift_right_logical(tl, 8)
    u = tl - 256 * grp
    tokv = jnp.where(u < 128, u, u - 64)
    valid = jnp.where(u < 128, 1, jnp.where(u >= 192, 1, 0))
    late = jnp.where(tokv >= SEG, 1, 0)
    segv = jnp.where(valid > 0, 2 * grp + late, -1)
    keptv = one(labv[...] != -100)
    spread = one(iota((SEG, 1024), 0) == tokv - SEG * late).astype(BF16)
    bd[...] = jnp.where(iota((8, 1024), 0) == segv, dot(keptv.astype(BF16), spread), 0.0)
    up8 = one(lax.shift_right_logical(iota((128, 16), 0), 3) == iota((128, 16), 1)).astype(BF16)
    up2 = one(lax.shift_right_logical(iota((32, 16), 0), 1) == iota((32, 16), 1)).astype(BF16)
    wide = one((iota((64, HALF), 1) & 63) == iota((64, HALF), 0)).astype(BF16)
    in8 = (iota((128, HALF), 0) & 7) == lax.shift_right_logical(iota((128, HALF), 1), 6)
    in2 = (iota((32, 128), 0) & 1) == lax.shift_right_logical(iota((32, 128), 1), 6)
    for c in range(2):
        pc = rp[c]
        a8 = dot(dot_nt(up8, pc).astype(BF16), wide)
        pm8[c] = jnp.where(in8, a8, 0.0).astype(BF16)
        a2 = dot(dot_nt(up2, pc).astype(BF16), wide[:, :128])
        pm2[c] = jnp.where(in2, a2, 0.0).astype(BF16)

    pl.semaphore_wait(tok.at[0], 2)
    for n in (-2, 2):
        pl.semaphore_signal(tok.at[1], inc=1, device_id=(z_off(n), f), device_id_type=MESH)

    total = zp[1, q]
    for i in reversed(range(7)):
        a1[i].wait_recv()
        total = total + ar[i]
    zf[k, q] = total
    a2 = [
        remote(zf.at[k, q], zf.at[k, q], s_a2.at[i], r_a2.at[i], (d, to * 2 + k))
        for i, (to, _) in enumerate(chips)
    ]
    for cp in a2:
        cp.start()
    fw = [None] * 8
    fw[7] = remote(zf.at[k, q], zf.at[k, q], s_fw.at[7], r_fw.at[7], twin)
    fw[7].start()
    pl.semaphore_wait(tok.at[1], 2)
    for n in (-4, 4):
        pl.semaphore_signal(tok.at[2], inc=1, device_id=(z_off(n), f), device_id_type=MESH)
    for i in reversed(range(7)):
        fro = chips[i][1]
        remote(zf.at[k, fro], zf.at[k, fro], s_a2.at[i], r_a2.at[i], twin).wait_recv()
        fw[i] = remote(zf.at[k, fro], zf.at[k, fro], s_fw.at[i], r_fw.at[i], twin)
        fw[i].start()

    def valid_features(c, at):
        lhs, rhs = [], []
        for g in range(4):
            za = zf[c, 2 * g : 2 * g + 2, 8].reshape(16, 128)
            zb = zf[c, 2 * g : 2 * g + 2, 7].reshape(16, 128)
            zg = jnp.concatenate([za, zb], axis=1)
            hi = zg.astype(BF16).astype(F32)
            lo = zg - hi
            mask = bd[:, 256 * g : 256 * g + 256]
            blocks = [
                jnp.broadcast_to(part[a : a + 1], (8, 256)) * mask
                for part in (hi, lo)
                for a in range(16)
            ]
            lhs.append(jnp.concatenate(blocks, axis=0).astype(BF16))
        left = []
        for n in range(2):
            cols = pl.ds(256 * n, 256)
            acc = None
            for g in range(4):
                rows = jnp.concatenate(
                    [
                        buf[1 - c, pl.ds(NT + 192 * g, 128), cols],
                        buf[1 - c, pl.ds(NT + 192 * g + 64, 128), cols],
                    ],
                    axis=0,
                )
                o = dot(lhs[g], rows)
                acc = o if acc is None else acc + o
            left.append(acc[:128] + acc[128:])
        hi, lo = split(jnp.concatenate(left, axis=1))
        o = dot(jnp.concatenate([hi, lo], axis=0), fp[c])
        o = o[:128] + o[128:]
        for h in range(2):
            part = o[:, 128 * h : 128 * h + 128].reshape(8, 2, 8, 128)
            for a2_ in range(2):
                pvl[at, :, 2 * a2_ + h] = part[:, a2_]

    def train_pair(c, i):
        t0 = (192 * i) // 128
        zg = jnp.concatenate(
            [zf[c, :, t0].reshape(64, 128), zf[c, :, t0 + 1].reshape(64, 128)], axis=1
        )
        cols = pl.ds(128 * t0, 256)
        lhs = jnp.concatenate(
            [zg * wt[2 * i : 2 * i + 1, cols], zg * wt[2 * i + 1 : 2 * i + 2, cols]], axis=0
        ).astype(BF16)
        for n in range(2):
            at = pl.ds(256 * n, 256)
            g2 = dot(lhs, buf[1 - c, pl.ds(128 * t0, 256), at])
            m = BETA_FIRST * m_[c, :, at]
            v = BETA_SECOND * v_[c, :, at]
            for s in range(2):
                g = g2[64 * s : 64 * s + 64]
                num = m + (1.0 - BETA_FIRST) * g
                second = v + (1.0 - BETA_SECOND) * g * g
                den = second * lax.rsqrt(second) + ADAM_EPS
                dirs[pl.ds(128 * i + 64 * s, 64), at] = (num / den).astype(BF16)

    def train_features(c, at):
        l8 = dot(pm8[c], dirs[pl.ds(0, 512), :])
        l2 = dot(pm2[c], dirs[pl.ds(512, 128), :])
        hi, lo = split(jnp.concatenate([l8, l2], axis=0))
        o = dot(jnp.concatenate([hi, lo], axis=0), fp[c])
        o = o[:160] + o[160:]
        for h in range(2):
            cols = o[:, 128 * h : 128 * h + 128]
            part = cols[:128].reshape(8, 2, 8, 128)
            for a2_ in range(2):
                ptl[at, :, 2 * a2_ + h] = part[:, a2_]
            for p in range(8):
                ptl[at, p, 4, pl.ds(4 * h, 4), :] = cols[128 + 4 * p : 132 + 4 * p]

    valid_features(k, 1)
    for i in range(8):
        at = q if i == 7 else chips[i][1]
        remote(
            zf.at[other, at], zf.at[other, at], s_fw.at[i], r_fw.at[i], twin
        ).wait_recv()
    valid_features(other, 0)
    tw_v = remote(pvl.at[0], pvtw, s_tw.at[1], r_tw.at[1], twin)
    tw_v.start()
    for i in range(5):
        train_pair(other, i)
        if i == 1:
            tw_v.wait_recv()
            pvl[1] = pvl[1] + pvtw[...]
            b_v = [
                remote(pvl.at[1, to], bvr.at[j], s_bv.at[j], r_bv.at[j], (d, to * 2 + k))
                for j, (to, _) in enumerate(chips)
            ]
            for cp in b_v:
                cp.start()
    train_features(other, 0)
    tw_t = remote(ptl.at[0], pttw, s_tw.at[2], r_tw.at[2], twin)
    tw_t.start()

    par = lax.rem(zm, 2)
    slot = lax.div(zm, 2) * 2 + zr
    mine = zr == par
    c_v = []
    for j in PAIR_OFFSETS:
        peer = (dp_at(y, 2 * lax.rem(zm + j, 8) + par), f)
        c_v.append(remote(vs, vg.at[slot], s_c.at[j], r_c.at[slot], peer))
    keep_v = pltpu.make_async_copy(vs, vg.at[slot], r_c.at[slot])

    for i in range(5):
        train_pair(k, i)
        if i == 2:
            pl.semaphore_wait(tok.at[2], 2)
            total = pvl[1, q]
            for j in reversed(range(7)):
                b_v[j].wait_recv()
                total = total + bvr[j]
            vs[...] = total
            for cp in c_v[:7]:
                cp.start()

            @pl.when(mine)
            def _():
                keep_v.start()

            @pl.when(jnp.logical_not(mine))
            def _():
                c_v[7].start()

    train_features(k, 1)
    tw_t.wait_recv()
    ptl[1] = ptl[1] + pttw[...]
    b_t = [
        remote(ptl.at[1, to], btr.at[j], s_bt.at[j], r_bt.at[j], (d, to * 2 + k))
        for j, (to, _) in enumerate(chips)
    ]
    for cp in b_t:
        cp.start()
    total = ptl[1, q]
    for j in reversed(range(7)):
        b_t[j].wait_recv()
        total = total + btr[j]
    ts[...] = total
    blk = 2 * y + zr
    tg[blk] = total
    partners = (
        (1 - y, zt, 2 * (1 - y) + 1 - zr),
        (1 - y, z, 2 * (1 - y) + zr),
        (y, zt, 2 * y + 1 - zr),
    )
    q_t = [
        remote(ts, tg.at[blk], s_q.at[j], r_q.at[j], (dp_at(py, pz), f))
        for j, (py, pz, _) in enumerate(partners)
    ]
    for cp in q_t:
        cp.start()
    for i in range(8):
        pltpu.make_async_copy(vs, vg.at[i], r_c.at[i]).wait()
    vals = jnp.concatenate([vg[:, t].reshape(64, 128) for t in range(4)], axis=1)
    ones = jnp.ones((8, HALF), F32)
    nv = dot_nt(ones, vals * vals, lax.Precision.HIGHEST)
    for j, (_, _, pb) in enumerate(partners):
        remote(ts, tg.at[pb], s_q.at[j], r_q.at[j], twin).wait_recv()

    tail = tg[:, 4].reshape(32, 128)
    row = iota((32, 128), 0) & 7
    quarter = 2 * (lax.shift_right_logical(row, 1) & 1) + lax.shift_right_logical(row, 2)
    lhs = []
    na = jnp.zeros((32, 1), F32)
    for t in range(4):
        top = tg[:, t].reshape(32, 128)
        na = na + jnp.sum(top * top, axis=1, keepdims=True)
        lhs.append(jnp.concatenate([top, jnp.where(quarter == t, tail, 0.0)], axis=0))
    nb = jnp.sum(tail * tail, axis=1, keepdims=True)
    cos = dot_nt(jnp.concatenate(lhs, axis=1), vals, lax.Precision.HIGHEST)
    nv4 = jnp.concatenate([nv] * 4, axis=0)
    half32 = lambda n: jnp.broadcast_to(n, (32, 32))
    msg_a = jnp.concatenate([cos[:32], nv4], axis=1)
    msg_b = jnp.concatenate([cos[32:], half32(na), half32(nb)], axis=1)
    ds[:, 0] = msg_a.reshape(4, 8, 128)
    ds[:, 1] = msg_b.reshape(4, 8, 128)
    d_c = []
    for by in range(2):
        for br in range(2):
            for i in range(4):
                to_f = 8 * y + 2 * i + zr
                b = 2 * by + br
                j = 4 * b + i
                here = jnp.logical_and(jnp.logical_and(y == by, zr == br), f == to_f)
                cp = remote(
                    ds.at[b], dr.at[f], s_d.at[j], r_d.at[f], (dp_at(by, 2 * zm + br), to_f)
                )
                keep = pltpu.make_async_copy(ds.at[b], dr.at[f], r_d.at[f])
                d_c.append((cp, here))

                @pl.when(jnp.logical_not(here))
                def _():
                    cp.start()

                @pl.when(here)
                def _():
                    keep.start()

    for cp in [tw_a, tw_v, tw_t] + a1 + a2 + fw + b_v + b_t + c_v[:7] + q_t:
        cp.wait_send()

    @pl.when(jnp.logical_not(mine))
    def _():
        c_v[7].wait_send()

    for i in range(16):
        pltpu.make_async_copy(ds.at[0], dr.at[i], r_d.at[i]).wait()
    sa = dr[0, 0]
    sb = dr[0, 1]
    for i in range(1, 16):
        sa = sa + dr[i, 0]
        sb = sb + dr[i, 1]
    inv_v = lax.rsqrt(sa[:, 64:128] + NORM_EPS)
    res_a = sa[:, 0:64] * lax.rsqrt(sb[:, 64:65] + NORM_EPS) * inv_v
    s2 = (sb[0:2] + sb[2:4]) + (sb[4:6] + sb[6:8])
    res_b = s2[:, 0:64] * lax.rsqrt(s2[:, 96:97] + NORM_EPS) * inv_v[0:2]
    pick = lax.rem(lax.div(f, 2), 4)
    for res, rows in ((res_a, pl.ds(0, 8)), (res_b, pl.ds(8, 2))):
        o = res[:, 0:16]
        for i in range(1, 4):
            o = jnp.where(pick == i, res[:, 16 * i : 16 * i + 16], o)
        out[rows, :] = o
    for cp, here in d_c:

        @pl.when(jnp.logical_not(here))
        def _():
            cp.wait_send()


def body(xt, ct, lt, xv, cv, lv, ad, au, mom1, mom2, rank_p, feat_p):
    dma = pltpu.SemaphoreType.DMA
    tile = lambda *lead: pltpu.VMEM(lead + (8, 128), F32)
    scratch = [
        pltpu.VMEM((2, NT + NV, HALF), BF16),
        pltpu.VMEM((2, 64, HALF), BF16),
        pltpu.VMEM((2, 64, 16), BF16),
        pltpu.VMEM((2, HALF, 256), BF16),
        pltpu.VMEM((2, 64, HALF), F32),
        pltpu.VMEM((2, 64, HALF), F32),
        pltpu.VMEM((10, SEG), jnp.int32),
        pltpu.VMEM((8, SEG), jnp.int32),
        tile(2, 8, 9),
        tile(8, 9),
        tile(7, 9),
        tile(2, 8, 9),
        pltpu.VMEM((16, 1024), F32),
        pltpu.VMEM((8, 1024), F32),
        pltpu.VMEM((2, 128, HALF), BF16),
        pltpu.VMEM((2, 32, 128), BF16),
        pltpu.VMEM((640, HALF), BF16),
        tile(2, 8, 4),
        tile(8, 4),
        tile(7, 4),
        tile(2, 8, 5),
        tile(8, 5),
        tile(7, 5),
        tile(4),
        tile(5),
        tile(8, 4),
        tile(4, 5),
        tile(4, 2),
        tile(16, 2),
        dma((12,)),
        dma((3,)), dma((3,)),
        dma((7,)), dma((7,)),
        dma((7,)), dma((7,)),
        dma((8,)), dma((8,)),
        dma((7,)), dma((7,)),
        dma((7,)), dma((7,)),
        dma((8,)), dma((8,)),
        dma((3,)), dma((3,)),
        dma((16,)), dma((16,)),
        pltpu.SemaphoreType.REGULAR((3,)),
    ]
    return pl.pallas_call(
        kernel,
        name="features",
        out_shape=jax.ShapeDtypeStruct((10, 16), F32),
        in_specs=[pl.BlockSpec(memory_space=pl.ANY)] * 12,
        out_specs=pl.BlockSpec(memory_space=pltpu.VMEM),
        scratch_shapes=scratch,
        compiler_params=pltpu.CompilerParams(
            collective_id=0, has_side_effects=True, vmem_limit_bytes=40 << 20
        ),
    )(
        xt.reshape(NT, HALF), ct.reshape(NT, HALF), lt,
        xv.reshape(NV, HALF), cv.reshape(NV, HALF), lv,
        ad, au, mom1, mom2, rank_p, feat_p,
    )


def solution(mesh):
    placed = (
        P("dp", None, "fsdp"),
        P("dp", None, "fsdp"),
        P("dp", None),
        P("dp", None, "fsdp"),
        P("dp", None, "fsdp"),
        P("dp", None),
        P(None, "fsdp"),
        P(None, "fsdp"),
        P(None, None, "fsdp"),
        P(None, None, "fsdp"),
        P(),
        P(None, "fsdp", None),
    )
    return jax.shard_map(
        body, mesh=mesh, in_specs=placed, out_specs=P("dp", "fsdp"), check_vma=False
    )
```

```python
import jax
import jax.numpy as jnp
from jax import lax
from jax.experimental import pallas as pl
from jax.experimental.pallas import tpu as pltpu
from jax.sharding import PartitionSpec as P

ADAPTER_SCALE = 2.0
BETA_FIRST = 0.9
BETA_SECOND = 0.999
ADAM_EPS = 1e-08
NORM_EPS = 1e-06

MESH = pl.DeviceIdType.MESH
F32 = jnp.float32
BF16 = jnp.bfloat16
SEG = 96
NT = 960
NV = 768
HALF = 512

OFFSETS = ((2, 1), (1, 1), (3, 1), (2, 0), (0, 1), (1, 0), (3, 0))
PAIR_OFFSETS = (4, 3, 5, 2, 6, 1, 7, 0)


def dot(a, b):
    return lax.dot_general(a, b, (((1,), (0,)), ((), ())), preferred_element_type=F32)


def dot_nt(a, b, precision=None):
    return lax.dot_general(
        a, b, (((1,), (1,)), ((), ())), preferred_element_type=F32, precision=precision
    )


def split(x):
    hi = x.astype(BF16)
    return hi, (x - hi.astype(F32)).astype(BF16)


def kernel(
    xt, ct, lt, xv, cv, lv, ad, au, mom1, mom2, rank_p, feat_p,
    out,
    buf, w, rp, fp, m_, v_, labt, labv,
    zp, ztw, ar, zf, wt, bd, pm8, pm2, dirs,
    pvl, pvtw, bvr, ptl, pttw, btr, vs, ts, vg, tg, ds, dr,
    ld, s_tw, r_tw, s_a1, r_a1, s_a2, r_a2, s_fw, r_fw, s_bv, r_bv, s_bt, r_bt,
    s_c, r_c, s_q, r_q, s_d, r_d, tok,
):
    d = lax.axis_index("dp")
    f = lax.axis_index("fsdp")
    y, z = lax.div(d, 16), lax.rem(d, 16)
    zm, zr = lax.div(z, 2), lax.rem(z, 2)
    q, k = lax.div(f, 2), lax.rem(f, 2)
    x, yh = lax.div(q, 2), lax.rem(q, 2)
    other = 1 - k
    twin = (d, f + 1 - 2 * k)
    chips = []
    for dx, dy in OFFSETS:
        to = lax.rem(x + dx, 4) * 2 + lax.rem(yh + dy, 2)
        fro = lax.rem(x + 4 - dx, 4) * 2 + lax.rem(yh + dy, 2)
        chips.append((to, fro))

    def dp_at(y_at, z_at):
        return y_at * 16 + z_at

    def z_off(n):
        return dp_at(y, lax.rem(z + n + 16, 16))

    loads = [
        (au, w.at[0]),
        (ad, w.at[1]),
        (rank_p, rp),
        (ct, buf.at[0, pl.ds(0, NT)]),
        (cv, buf.at[0, pl.ds(NT, NV)]),
        (xt, buf.at[1, pl.ds(0, NT)]),
        (xv, buf.at[1, pl.ds(NT, NV)]),
        (lt, labt),
        (lv, labv),
        (feat_p, fp),
        (mom1, m_),
        (mom2, v_),
    ]
    load = [pltpu.make_async_copy(a, b, ld.at[i]) for i, (a, b) in enumerate(loads)]
    for cp in load:
        cp.start()

    barrier = pltpu.get_barrier_semaphore()
    zt = z + 1 - 2 * zr
    greet = [(d, to * 2 + k) for to, _ in chips]
    greet += [twin, (dp_at(1 - y, z), f), (dp_at(y, zt), f), (dp_at(1 - y, zt), f)]
    greet += [(dp_at(y, lax.rem(z + 15 + 2 * zr, 16)), f)]
    for peer in greet:
        pl.semaphore_signal(barrier, inc=1, device_id=peer, device_id_type=MESH)

    def remote(src, dst, send, recv, peer):
        return pltpu.make_async_remote_copy(
            src_ref=src, dst_ref=dst, send_sem=send, recv_sem=recv,
            device_id=peer, device_id_type=MESH,
        )

    def arrived(src, dst, sem):
        pltpu.make_async_copy(src, dst, sem).wait()

    lane = lax.broadcasted_iota(jnp.int32, (16, 128), 1)

    def inner(c, at):
        wc = w[c]
        hi, lo = split(dot(rp[c], wc))
        both = jnp.concatenate([hi, lo], axis=0)
        for t in range(4):
            o = dot_nt(wc, buf[c, pl.ds(256 * t, 256), :])
            zp[at, :, 2 * t] = o[:, :128].reshape(8, 8, 128)
            if t < 3:
                zp[at, :, 2 * t + 1] = o[:, 128:].reshape(8, 8, 128)
            else:
                tail = o[:, 128:]
        for g in range(4):
            rows = jnp.concatenate(
                [
                    buf[c, pl.ds(NT + 192 * g, 128), :],
                    buf[c, pl.ds(NT + 192 * g + 64, 128), :],
                ],
                axis=0,
            )
            o = dot_nt(both, rows)
            o = o[:16] + o[16:]
            zp[at, 2 * g : 2 * g + 2, 8] = o[:, :128].reshape(2, 8, 128)
            mixed = jnp.where(lane < 64, tail[16 * g : 16 * g + 16], o[:, 128:])
            zp[at, 2 * g : 2 * g + 2, 7] = mixed.reshape(2, 8, 128)

    for i in range(7):
        load[i].wait()
    inner(other, 0)
    pl.semaphore_wait(barrier, len(greet))
    tw_a = remote(zp.at[0], ztw, s_tw.at[0], r_tw.at[0], twin)
    tw_a.start()
    for n in (-1, 1):
        pl.semaphore_signal(tok.at[0], inc=1, device_id=(z_off(n), f), device_id_type=MESH)
    inner(k, 1)
    tw_a.wait_recv()
    zp[1] = zp[1] + ztw[...]
    a1 = [
        remote(zp.at[1, to], ar.at[i], s_a1.at[i], r_a1.at[i], (d, to * 2 + k))
        for i, (to, _) in enumerate(chips)
    ]
    for cp in a1:
        cp.start()

    for i in range(7, 12):
        load[i].wait()
    iota = lambda shape, dim: lax.broadcasted_iota(jnp.int32, shape, dim)
    one = lambda cond: jnp.where(cond, 1.0, 0.0)
    tl = iota((1, 1024), 1)
    seg = jnp.zeros((1, 1024), jnp.int32)
    for j in range(1, 11):
        seg = seg + jnp.where(tl >= SEG * j, 1, 0)
    kept = one(labt[...] != -100)
    scale = ADAPTER_SCALE / jnp.sum(kept, axis=1, keepdims=True)
    spread = one(iota((SEG, 1024), 0) == tl - SEG * seg).astype(BF16)
    laid = dot(kept.astype(BF16), spread)
    wt[0:10, :] = jnp.where(iota((10, 1024), 0) == seg, laid * scale, 0.0)
    grp = lax.shift_right_logical(tl, 8)
    u = tl - 256 * grp
    tokv = jnp.where(u < 128, u, u - 64)
    valid = jnp.where(u < 128, 1, jnp.where(u >= 192, 1, 0))
    late = jnp.where(tokv >= SEG, 1, 0)
    segv = jnp.where(valid > 0, 2 * grp + late, -1)
    keptv = one(labv[...] != -100)
    spread = one(iota((SEG, 1024), 0) == tokv - SEG * late).astype(BF16)
    bd[...] = jnp.where(iota((8, 1024), 0) == segv, dot(keptv.astype(BF16), spread), 0.0)
    up8 = one(lax.shift_right_logical(iota((128, 16), 0), 3) == iota((128, 16), 1)).astype(BF16)
    up2 = one(lax.shift_right_logical(iota((32, 16), 0), 1) == iota((32, 16), 1)).astype(BF16)
    wide = one((iota((64, HALF), 1) & 63) == iota((64, HALF), 0)).astype(BF16)
    in8 = (iota((128, HALF), 0) & 7) == lax.shift_right_logical(iota((128, HALF), 1), 6)
    in2 = (iota((32, 128), 0) & 1) == lax.shift_right_logical(iota((32, 128), 1), 6)
    for c in range(2):
        pc = rp[c]
        a8 = dot(dot(up8, pc).astype(BF16), wide)
        pm8[c] = jnp.where(in8, a8, 0.0).astype(BF16)
        a2 = dot(dot(up2, pc).astype(BF16), wide[:, :128])
        pm2[c] = jnp.where(in2, a2, 0.0).astype(BF16)

    pl.semaphore_wait(tok.at[0], 2)
    for n in (-2, 2):
        pl.semaphore_signal(tok.at[1], inc=1, device_id=(z_off(n), f), device_id_type=MESH)

    total = zp[1, q]
    for i in reversed(range(7)):
        a1[i].wait_recv()
        total = total + ar[i]
    zf[k, q] = total
    a2 = [
        remote(zf.at[k, q], zf.at[k, q], s_a2.at[i], r_a2.at[i], (d, to * 2 + k))
        for i, (to, _) in enumerate(chips)
    ]
    for cp in a2:
        cp.start()
    fw = [None] * 8
    fw[7] = remote(zf.at[k, q], zf.at[k, q], s_fw.at[7], r_fw.at[7], twin)
    fw[7].start()
    pl.semaphore_wait(tok.at[1], 2)
    for n in (-4, 4):
        pl.semaphore_signal(tok.at[2], inc=1, device_id=(z_off(n), f), device_id_type=MESH)
    for i in reversed(range(7)):
        fro = chips[i][1]
        remote(zf.at[k, fro], zf.at[k, fro], s_a2.at[i], r_a2.at[i], twin).wait_recv()
        fw[i] = remote(zf.at[k, fro], zf.at[k, fro], s_fw.at[i], r_fw.at[i], twin)
        fw[i].start()

    def valid_features(c, at):
        lhs, rhs = [], []
        for g in range(4):
            za = zf[c, 2 * g : 2 * g + 2, 8].reshape(16, 128)
            zb = zf[c, 2 * g : 2 * g + 2, 7].reshape(16, 128)
            zg = jnp.concatenate([za, zb], axis=1)
            hi = zg.astype(BF16).astype(F32)
            lo = zg - hi
            mask = bd[:, 256 * g : 256 * g + 256]
            blocks = [
                jnp.broadcast_to(part[a : a + 1], (8, 256)) * mask
                for part in (hi, lo)
                for a in range(16)
            ]
            lhs.append(jnp.concatenate(blocks, axis=0).astype(BF16))
        left = []
        for n in range(2):
            cols = pl.ds(256 * n, 256)
            acc = None
            for g in range(4):
                rows = jnp.concatenate(
                    [
                        buf[1 - c, pl.ds(NT + 192 * g, 128), cols],
                        buf[1 - c, pl.ds(NT + 192 * g + 64, 128), cols],
                    ],
                    axis=0,
                )
                o = dot(lhs[g], rows)
                acc = o if acc is None else acc + o
            left.append(acc[:128] + acc[128:])
        hi, lo = split(jnp.concatenate(left, axis=1))
        o = dot(jnp.concatenate([hi, lo], axis=0), fp[c])
        o = o[:128] + o[128:]
        for h in range(2):
            part = o[:, 128 * h : 128 * h + 128].reshape(8, 2, 8, 128)
            for a2_ in range(2):
                pvl[at, :, 2 * a2_ + h] = part[:, a2_]

    def train_pair(c, i):
        t0 = (192 * i) // 128
        zg = jnp.concatenate(
            [zf[c, :, t0].reshape(64, 128), zf[c, :, t0 + 1].reshape(64, 128)], axis=1
        )
        cols = pl.ds(128 * t0, 256)
        lhs = jnp.concatenate(
            [zg * wt[2 * i : 2 * i + 1, cols], zg * wt[2 * i + 1 : 2 * i + 2, cols]], axis=0
        ).astype(BF16)
        for n in range(2):
            at = pl.ds(256 * n, 256)
            g2 = dot(lhs, buf[1 - c, pl.ds(128 * t0, 256), at])
            m = BETA_FIRST * m_[c, :, at]
            v = BETA_SECOND * v_[c, :, at]
            for s in range(2):
                g = g2[64 * s : 64 * s + 64]
                num = m + (1.0 - BETA_FIRST) * g
                second = v + (1.0 - BETA_SECOND) * g * g
                den = second * lax.rsqrt(second) + ADAM_EPS
                dirs[pl.ds(128 * i + 64 * s, 64), at] = (num / den).astype(BF16)

    def train_features(c, at):
        l8 = dot(pm8[c], dirs[pl.ds(0, 512), :])
        l2 = dot(pm2[c], dirs[pl.ds(512, 128), :])
        hi, lo = split(jnp.concatenate([l8, l2], axis=0))
        o = dot(jnp.concatenate([hi, lo], axis=0), fp[c])
        o = o[:160] + o[160:]
        for h in range(2):
            cols = o[:, 128 * h : 128 * h + 128]
            part = cols[:128].reshape(8, 2, 8, 128)
            for a2_ in range(2):
                ptl[at, :, 2 * a2_ + h] = part[:, a2_]
            for p in range(8):
                ptl[at, p, 4, pl.ds(4 * h, 4), :] = cols[128 + 4 * p : 132 + 4 * p]

    valid_features(k, 1)
    for i in range(8):
        at = q if i == 7 else chips[i][1]
        remote(
            zf.at[other, at], zf.at[other, at], s_fw.at[i], r_fw.at[i], twin
        ).wait_recv()
    valid_features(other, 0)
    tw_v = remote(pvl.at[0], pvtw, s_tw.at[1], r_tw.at[1], twin)
    tw_v.start()
    for i in range(5):
        train_pair(other, i)
        if i == 1:
            tw_v.wait_recv()
            pvl[1] = pvl[1] + pvtw[...]
            b_v = [
                remote(pvl.at[1, to], bvr.at[j], s_bv.at[j], r_bv.at[j], (d, to * 2 + k))
                for j, (to, _) in enumerate(chips)
            ]
            for cp in b_v:
                cp.start()
    train_features(other, 0)
    tw_t = remote(ptl.at[0], pttw, s_tw.at[2], r_tw.at[2], twin)
    tw_t.start()

    par = lax.rem(zm, 2)
    slot = lax.div(zm, 2) * 2 + zr
    mine = zr == par
    c_v = []
    for j in PAIR_OFFSETS:
        peer = (dp_at(y, 2 * lax.rem(zm + j, 8) + par), f)
        c_v.append(remote(vs, vg.at[slot], s_c.at[j], r_c.at[slot], peer))
    keep_v = pltpu.make_async_copy(vs, vg.at[slot], r_c.at[slot])

    for i in range(5):
        train_pair(k, i)
        if i == 2:
            pl.semaphore_wait(tok.at[2], 2)
            total = pvl[1, q]
            for j in reversed(range(7)):
                b_v[j].wait_recv()
                total = total + bvr[j]
            vs[...] = total
            for cp in c_v[:7]:
                cp.start()

            @pl.when(mine)
            def _():
                keep_v.start()

            @pl.when(jnp.logical_not(mine))
            def _():
                c_v[7].start()

    train_features(k, 1)
    tw_t.wait_recv()
    ptl[1] = ptl[1] + pttw[...]
    b_t = [
        remote(ptl.at[1, to], btr.at[j], s_bt.at[j], r_bt.at[j], (d, to * 2 + k))
        for j, (to, _) in enumerate(chips)
    ]
    for cp in b_t:
        cp.start()
    total = ptl[1, q]
    for j in reversed(range(7)):
        b_t[j].wait_recv()
        total = total + btr[j]
    ts[...] = total
    blk = 2 * y + zr
    tg[blk] = total
    partners = (
        (1 - y, zt, 2 * (1 - y) + 1 - zr),
        (1 - y, z, 2 * (1 - y) + zr),
        (y, zt, 2 * y + 1 - zr),
    )
    q_t = [
        remote(ts, tg.at[blk], s_q.at[j], r_q.at[j], (dp_at(py, pz), f))
        for j, (py, pz, _) in enumerate(partners)
    ]
    for cp in q_t:
        cp.start()
    for i in range(8):
        arrived(vs, vg.at[i], r_c.at[i])
    vals = jnp.concatenate([vg[:, t].reshape(64, 128) for t in range(4)], axis=1)
    ones = jnp.ones((8, HALF), F32)
    nv = dot_nt(ones, vals * vals, lax.Precision.HIGHEST)
    for j, (_, _, pb) in enumerate(partners):
        remote(ts, tg.at[pb], s_q.at[j], r_q.at[j], twin).wait_recv()

    tail = tg[:, 4].reshape(32, 128)
    row = iota((32, 128), 0) & 7
    quarter = 2 * (lax.shift_right_logical(row, 1) & 1) + lax.shift_right_logical(row, 2)
    lhs = []
    na = jnp.zeros((32, 1), F32)
    for t in range(4):
        top = tg[:, t].reshape(32, 128)
        na = na + jnp.sum(top * top, axis=1, keepdims=True)
        lhs.append(jnp.concatenate([top, jnp.where(quarter == t, tail, 0.0)], axis=0))
    nb = jnp.sum(tail * tail, axis=1, keepdims=True)
    cos = dot_nt(jnp.concatenate(lhs, axis=1), vals, lax.Precision.HIGHEST)
    nv4 = jnp.concatenate([nv] * 4, axis=0)
    half32 = lambda n: jnp.broadcast_to(n, (32, 32))
    msg_a = jnp.concatenate([cos[:32], nv4], axis=1)
    msg_b = jnp.concatenate([cos[32:], half32(na), half32(nb)], axis=1)
    ds[:, 0] = msg_a.reshape(4, 8, 128)
    ds[:, 1] = msg_b.reshape(4, 8, 128)
    d_c = []
    for by in range(2):
        for br in range(2):
            for i in range(4):
                to_f = 8 * y + 2 * i + zr
                b = 2 * by + br
                j = 4 * b + i
                here = jnp.logical_and(jnp.logical_and(y == by, zr == br), f == to_f)
                cp = remote(
                    ds.at[b], dr.at[f], s_d.at[j], r_d.at[f], (dp_at(by, 2 * zm + br), to_f)
                )
                keep = pltpu.make_async_copy(ds.at[b], dr.at[f], r_d.at[f])
                d_c.append((cp, here))

                @pl.when(jnp.logical_not(here))
                def _():
                    cp.start()

                @pl.when(here)
                def _():
                    keep.start()

    for cp in [tw_a, tw_v, tw_t] + a1 + a2 + fw + b_v + b_t + c_v[:7] + q_t:
        cp.wait_send()

    @pl.when(jnp.logical_not(mine))
    def _():
        c_v[7].wait_send()

    for i in range(16):
        arrived(ds.at[0], dr.at[i], r_d.at[i])
    sa = dr[0, 0]
    sb = dr[0, 1]
    for i in range(1, 16):
        sa = sa + dr[i, 0]
        sb = sb + dr[i, 1]
    inv_v = lax.rsqrt(sa[:, 64:128] + NORM_EPS)
    res_a = sa[:, 0:64] * lax.rsqrt(sb[:, 64:65] + NORM_EPS) * inv_v
    s2 = (sb[0:2] + sb[2:4]) + (sb[4:6] + sb[6:8])
    res_b = s2[:, 0:64] * lax.rsqrt(s2[:, 96:97] + NORM_EPS) * inv_v[0:2]
    pick = lax.rem(lax.div(f, 2), 4)
    for res, rows in ((res_a, pl.ds(0, 8)), (res_b, pl.ds(8, 2))):
        o = res[:, 0:16]
        for i in range(1, 4):
            o = jnp.where(pick == i, res[:, 16 * i : 16 * i + 16], o)
        out[rows, :] = o
    for cp, here in d_c:

        @pl.when(jnp.logical_not(here))
        def _():
            cp.wait_send()


def body(xt, ct, lt, xv, cv, lv, ad, au, mom1, mom2, rank_p, feat_p):
    dma = pltpu.SemaphoreType.DMA
    tile = lambda *lead: pltpu.VMEM(lead + (8, 128), F32)
    scratch = [
        pltpu.VMEM((2, NT + NV, HALF), BF16),
        pltpu.VMEM((2, 64, HALF), BF16),
        pltpu.VMEM((2, 16, 64), BF16),
        pltpu.VMEM((2, HALF, 256), BF16),
        pltpu.VMEM((2, 64, HALF), F32),
        pltpu.VMEM((2, 64, HALF), F32),
        pltpu.VMEM((10, SEG), jnp.int32),
        pltpu.VMEM((8, SEG), jnp.int32),
        tile(2, 8, 9),
        tile(8, 9),
        tile(7, 9),
        tile(2, 8, 9),
        pltpu.VMEM((16, 1024), F32),
        pltpu.VMEM((8, 1024), F32),
        pltpu.VMEM((2, 128, HALF), BF16),
        pltpu.VMEM((2, 32, 128), BF16),
        pltpu.VMEM((640, HALF), BF16),
        tile(2, 8, 4),
        tile(8, 4),
        tile(7, 4),
        tile(2, 8, 5),
        tile(8, 5),
        tile(7, 5),
        tile(4),
        tile(5),
        tile(8, 4),
        tile(4, 5),
        tile(4, 2),
        tile(16, 2),
        dma((12,)),
        dma((3,)), dma((3,)),
        dma((7,)), dma((7,)),
        dma((7,)), dma((7,)),
        dma((8,)), dma((8,)),
        dma((7,)), dma((7,)),
        dma((7,)), dma((7,)),
        dma((8,)), dma((8,)),
        dma((3,)), dma((3,)),
        dma((16,)), dma((16,)),
        pltpu.SemaphoreType.REGULAR((3,)),
    ]
    return pl.pallas_call(
        kernel,
        name="features",
        out_shape=jax.ShapeDtypeStruct((10, 16), F32),
        in_specs=[pl.BlockSpec(memory_space=pltpu.HBM)] * 12,
        out_specs=pl.BlockSpec(memory_space=pltpu.VMEM),
        scratch_shapes=scratch,
        compiler_params=pltpu.CompilerParams(
            collective_id=0, has_side_effects=True, vmem_limit_bytes=60 << 20
        ),
    )(
        xt.reshape(NT, HALF), ct.reshape(NT, HALF), lt,
        xv.reshape(NV, HALF), cv.reshape(NV, HALF), lv,
        ad, au, mom1, mom2, jnp.swapaxes(rank_p, 1, 2), feat_p,
    )


def solution(mesh):
    placed = (
        P("dp", None, "fsdp"),
        P("dp", None, "fsdp"),
        P("dp", None),
        P("dp", None, "fsdp"),
        P("dp", None, "fsdp"),
        P("dp", None),
        P(None, "fsdp"),
        P(None, "fsdp"),
        P(None, None, "fsdp"),
        P(None, None, "fsdp"),
        P(),
        P(None, "fsdp", None),
    )
    return jax.shard_map(
        body, mesh=mesh, in_specs=placed, out_specs=P("dp", "fsdp"), check_vma=False
    )
```

```python
import jax
import jax.numpy as jnp
from jax import lax
from jax.experimental import pallas as pl
from jax.experimental.pallas import tpu as pltpu
from jax.sharding import PartitionSpec as P

ADAPTER_SCALE = 2.0
BETA_FIRST = 0.9
BETA_SECOND = 0.999
ADAM_EPS = 1e-08
NORM_EPS = 1e-06

MESH = pl.DeviceIdType.MESH
F32 = jnp.float32
BF16 = jnp.bfloat16
SEG = 96
NT = 960
NV = 768
HALF = 512

OFFSETS = ((2, 1), (1, 1), (3, 1), (2, 0), (0, 1), (1, 0), (3, 0))
PAIR_OFFSETS = (4, 3, 5, 2, 6, 1, 7, 0)


def dot(a, b):
    return lax.dot_general(a, b, (((1,), (0,)), ((), ())), preferred_element_type=F32)


def dot_nt(a, b, precision=None):
    return lax.dot_general(
        a, b, (((1,), (1,)), ((), ())), preferred_element_type=F32, precision=precision
    )


def split(x):
    hi = x.astype(BF16)
    return hi, (x - hi.astype(F32)).astype(BF16)


def kernel(
    xt, ct, lt, xv, cv, lv, ad, au, mom1, mom2, rank_p, feat_p,
    out,
    buf, w, rp, fp, m_, v_, labt, labv,
    zv, zvtw, arv, zfv, zt, zttw, art, zft, wt, bd, pm8, pm2, dirs,
    pvl, pvtw, bvr, ptl, pttw, btr, vs, ts, vg, tg, ds, dr,
    ld, la, s_tw, r_tw, s_a1v, r_a1v, s_a2v, r_a2v, s_fwv, r_fwv,
    s_a1t, r_a1t, s_a2t, r_a2t, s_fwt, r_fwt, s_bv, r_bv, s_bt, r_bt,
    s_c, r_c, s_q, r_q, s_d, r_d, tok,
):
    d = lax.axis_index("dp")
    f = lax.axis_index("fsdp")
    y, z = lax.div(d, 16), lax.rem(d, 16)
    zm, zr = lax.div(z, 2), lax.rem(z, 2)
    q, k = lax.div(f, 2), lax.rem(f, 2)
    x, yh = lax.div(q, 2), lax.rem(q, 2)
    other = 1 - k
    twin = (d, f + 1 - 2 * k)
    chips = []
    for dx, dy in OFFSETS:
        to = lax.rem(x + dx, 4) * 2 + lax.rem(yh + dy, 2)
        fro = lax.rem(x + 4 - dx, 4) * 2 + lax.rem(yh + dy, 2)
        chips.append((to, fro))

    def dp_at(y_at, z_at):
        return y_at * 16 + z_at

    def z_off(n):
        return dp_at(y, lax.rem(z + n + 16, 16))

    barrier = pltpu.get_barrier_semaphore()
    zo = z + 1 - 2 * zr
    greet = [(d, to * 2 + k) for to, _ in chips]
    greet += [twin, (dp_at(1 - y, z), f), (dp_at(y, zo), f), (dp_at(1 - y, zo), f)]
    greet += [(dp_at(y, lax.rem(z + 15 + 2 * zr, 16)), f)]
    for peer in greet:
        pl.semaphore_signal(barrier, inc=1, device_id=peer, device_id_type=MESH)

    last = 896
    loads = (
        (au, w.at[0]),
        (ad, w.at[1]),
        (rank_p, rp),
        (lt, labt),
        (lv, labv),
        (feat_p, fp),
        (mom1, m_),
        (mom2, v_),
    )
    load = [pltpu.make_async_copy(a, b, ld.at[i]) for i, (a, b) in enumerate(loads)]
    acts = []
    for c, (tr, va) in enumerate(((ct, cv), (xt, xv))):
        acts.append(
            [
                pltpu.make_async_copy(a, buf.at[c, pl.ds(to, n)], la.at[c, i])
                for i, (a, to, n) in enumerate(
                    (
                        (va, NT, NV),
                        (tr.at[pl.ds(last, NT - last)], last, NT - last),
                        (tr.at[pl.ds(0, last)], 0, last),
                    )
                )
            ]
        )
    for cp in load[:3]:
        cp.start()
    for mine_k in range(2):

        @pl.when(k == mine_k)
        def _():
            for i in (0, 1, 2):
                for c in (1 - mine_k, mine_k):
                    acts[c][i].start()

    for cp in load[3:]:
        cp.start()

    def loaded(c, i):
        src = xt.at[pl.ds(0, (NV, NT - last, last)[i])] if i else xv
        at = (NT, last, 0)[i]
        pltpu.make_async_copy(
            src, buf.at[c, pl.ds(at, (NV, NT - last, last)[i])], la.at[c, i]
        ).wait()

    def remote(src, dst, send, recv, peer):
        return pltpu.make_async_remote_copy(
            src_ref=src, dst_ref=dst, send_sem=send, recv_sem=recv,
            device_id=peer, device_id_type=MESH,
        )

    def arrived(src, dst, sem):
        pltpu.make_async_copy(src, dst, sem).wait()

    lane = lax.broadcasted_iota(jnp.int32, (16, 128), 1)

    def inner_valid(c, at):
        wc = w[c]
        hi, lo = split(dot(rp[c], wc))
        both = jnp.concatenate([hi, lo], axis=0)
        tail = dot_nt(wc, buf[c, pl.ds(last, 128), :])
        for g in range(4):
            rows = jnp.concatenate(
                [
                    buf[c, pl.ds(NT + 192 * g, 128), :],
                    buf[c, pl.ds(NT + 192 * g + 64, 128), :],
                ],
                axis=0,
            )
            o = dot_nt(both, rows)
            o = o[:16] + o[16:]
            zv[at, 2 * g : 2 * g + 2, 1] = o[:, :128].reshape(2, 8, 128)
            mixed = jnp.where(lane < 64, tail[16 * g : 16 * g + 16], o[:, 128:])
            zv[at, 2 * g : 2 * g + 2, 0] = mixed.reshape(2, 8, 128)

    def inner_train(c, at):
        wc = w[c]
        for t in range(4):
            n = 256 if t < 3 else 128
            o = dot_nt(wc, buf[c, pl.ds(256 * t, n), :])
            for j in range(n // 128):
                zt[at, :, 2 * t + j] = o[:, 128 * j : 128 * j + 128].reshape(8, 8, 128)

    def to_chips(src, dst, send, recv):
        cps = [
            remote(src(to), dst(i), send.at[i], recv.at[i], (d, to * 2 + k))
            for i, (to, _) in enumerate(chips)
        ]
        for cp in cps:
            cp.start()
        return cps

    for i in range(3):
        load[i].wait()
    for c in (other, k):
        loaded(c, 0)
        loaded(c, 1)
        inner_valid(c, 0) if c is other else inner_valid(c, 1)
        if c is other:
            pl.semaphore_wait(barrier, len(greet))
            tw_av = remote(zv.at[0], zvtw, s_tw.at[0], r_tw.at[0], twin)
            tw_av.start()
            for n in (-1, 1):
                pl.semaphore_signal(
                    tok.at[0], inc=1, device_id=(z_off(n), f), device_id_type=MESH
                )
    loaded(other, 2)
    inner_train(other, 0)
    tw_at = remote(zt.at[0], zttw, s_tw.at[3], r_tw.at[3], twin)
    tw_at.start()
    tw_av.wait_recv()
    zv[1] = zv[1] + zvtw[...]
    a1v = to_chips(lambda to: zv.at[1, to], lambda i: arv.at[i], s_a1v, r_a1v)
    loaded(k, 2)
    inner_train(k, 1)
    tw_at.wait_recv()
    zt[1] = zt[1] + zttw[...]
    a1t = to_chips(lambda to: zt.at[1, to], lambda i: art.at[i], s_a1t, r_a1t)

    for cp in load[3:]:
        cp.wait()
    iota = lambda shape, dim: lax.broadcasted_iota(jnp.int32, shape, dim)
    one = lambda cond: jnp.where(cond, 1.0, 0.0)
    tl = iota((1, 1024), 1)
    seg = jnp.zeros((1, 1024), jnp.int32)
    for j in range(1, 11):
        seg = seg + jnp.where(tl >= SEG * j, 1, 0)
    kept = one(labt[...] != -100)
    scale = ADAPTER_SCALE / jnp.sum(kept, axis=1, keepdims=True)
    spread = one(iota((SEG, 1024), 0) == tl - SEG * seg).astype(BF16)
    laid = dot(kept.astype(BF16), spread)
    wt[0:10, :] = jnp.where(iota((10, 1024), 0) == seg, laid * scale, 0.0)
    grp = lax.shift_right_logical(tl, 8)
    u = tl - 256 * grp
    tokv = jnp.where(u < 128, u, u - 64)
    valid = jnp.where(u < 128, 1, jnp.where(u >= 192, 1, 0))
    late = jnp.where(tokv >= SEG, 1, 0)
    segv = jnp.where(valid > 0, 2 * grp + late, -1)
    keptv = one(labv[...] != -100)
    spread = one(iota((SEG, 1024), 0) == tokv - SEG * late).astype(BF16)
    bd[...] = jnp.where(iota((8, 1024), 0) == segv, dot(keptv.astype(BF16), spread), 0.0)
    up8 = one(lax.shift_right_logical(iota((128, 16), 0), 3) == iota((128, 16), 1)).astype(BF16)
    up2 = one(lax.shift_right_logical(iota((32, 16), 0), 1) == iota((32, 16), 1)).astype(BF16)
    wide = one((iota((64, HALF), 1) & 63) == iota((64, HALF), 0)).astype(BF16)
    in8 = (iota((128, HALF), 0) & 7) == lax.shift_right_logical(iota((128, HALF), 1), 6)
    in2 = (iota((32, 128), 0) & 1) == lax.shift_right_logical(iota((32, 128), 1), 6)
    for c in range(2):
        pc = rp[c]
        a8 = dot(dot(up8, pc).astype(BF16), wide)
        pm8[c] = jnp.where(in8, a8, 0.0).astype(BF16)
        a2 = dot(dot(up2, pc).astype(BF16), wide[:, :128])
        pm2[c] = jnp.where(in2, a2, 0.0).astype(BF16)

    pl.semaphore_wait(tok.at[0], 2)
    for n in (-2, 2):
        pl.semaphore_signal(tok.at[1], inc=1, device_id=(z_off(n), f), device_id_type=MESH)

    def summed(own, cps, parts):
        total = own
        for i in reversed(range(7)):
            cps[i].wait_recv()
            total = total + parts[i]
        return total

    def spread_out(zf, send, recv, fsend, frecv):
        cps = to_chips(lambda to: zf.at[k, q], lambda i: zf.at[k, q], send, recv)
        cp = remote(zf.at[k, q], zf.at[k, q], fsend.at[7], frecv.at[7], twin)
        cp.start()
        return cps + [cp]

    def forward(zf, send, recv, fsend, frecv):
        cps = []
        for i in reversed(range(7)):
            fro = chips[i][1]
            at = zf.at[k, fro]
            remote(at, at, send.at[i], recv.at[i], twin).wait_recv()
            cps.append(remote(at, at, fsend.at[i], frecv.at[i], twin))
            cps[-1].start()
        return cps

    def forwarded(zf, fsend, frecv):
        for i in range(8):
            at = zf.at[other, q if i == 7 else chips[i][1]]
            remote(at, at, fsend.at[i], frecv.at[i], twin).wait_recv()

    zfv[k, q] = summed(zv[1, q], a1v, arv)
    a2v = spread_out(zfv, s_a2v, r_a2v, s_fwv, r_fwv)
    zft[k, q] = summed(zt[1, q], a1t, art)
    a2t = spread_out(zft, s_a2t, r_a2t, s_fwt, r_fwt)
    pl.semaphore_wait(tok.at[1], 2)
    for n in (-4, 4):
        pl.semaphore_signal(tok.at[2], inc=1, device_id=(z_off(n), f), device_id_type=MESH)
    a2v += forward(zfv, s_a2v, r_a2v, s_fwv, r_fwv)

    def valid_features(c, at):
        lhs, rhs = [], []
        for g in range(4):
            za = zfv[c, 2 * g : 2 * g + 2, 1].reshape(16, 128)
            zb = zfv[c, 2 * g : 2 * g + 2, 0].reshape(16, 128)
            zg = jnp.concatenate([za, zb], axis=1)
            hi = zg.astype(BF16).astype(F32)
            lo = zg - hi
            mask = bd[:, 256 * g : 256 * g + 256]
            blocks = [
                jnp.broadcast_to(part[a : a + 1], (8, 256)) * mask
                for part in (hi, lo)
                for a in range(16)
            ]
            lhs.append(jnp.concatenate(blocks, axis=0).astype(BF16))
        left = []
        for n in range(2):
            cols = pl.ds(256 * n, 256)
            acc = None
            for g in range(4):
                rows = jnp.concatenate(
                    [
                        buf[1 - c, pl.ds(NT + 192 * g, 128), cols],
                        buf[1 - c, pl.ds(NT + 192 * g + 64, 128), cols],
                    ],
                    axis=0,
                )
                o = dot(lhs[g], rows)
                acc = o if acc is None else acc + o
            left.append(acc[:128] + acc[128:])
        hi, lo = split(jnp.concatenate(left, axis=1))
        o = dot(jnp.concatenate([hi, lo], axis=0), fp[c])
        o = o[:128] + o[128:]
        for h in range(2):
            part = o[:, 128 * h : 128 * h + 128].reshape(8, 2, 8, 128)
            for a2_ in range(2):
                pvl[at, :, 2 * a2_ + h] = part[:, a2_]

    def train_pair(c, i):
        t0 = (192 * i) // 128
        second = zft[c, :, t0 + 1] if t0 < 6 else zfv[c, :, 0]
        zg = jnp.concatenate([zft[c, :, t0].reshape(64, 128), second.reshape(64, 128)], axis=1)
        cols = pl.ds(128 * t0, 256)
        lhs = jnp.concatenate(
            [zg * wt[2 * i : 2 * i + 1, cols], zg * wt[2 * i + 1 : 2 * i + 2, cols]], axis=0
        ).astype(BF16)
        for n in range(2):
            at = pl.ds(256 * n, 256)
            g2 = dot(lhs, buf[1 - c, pl.ds(128 * t0, 256), at])
            m = BETA_FIRST * m_[c, :, at]
            v = BETA_SECOND * v_[c, :, at]
            for s in range(2):
                g = g2[64 * s : 64 * s + 64]
                num = m + (1.0 - BETA_FIRST) * g
                second = v + (1.0 - BETA_SECOND) * g * g
                den = second * lax.rsqrt(second) + ADAM_EPS
                dirs[pl.ds(128 * i + 64 * s, 64), at] = (num / den).astype(BF16)

    def train_features(c, at):
        l8 = dot(pm8[c], dirs[pl.ds(0, 512), :])
        l2 = dot(pm2[c], dirs[pl.ds(512, 128), :])
        hi, lo = split(jnp.concatenate([l8, l2], axis=0))
        o = dot(jnp.concatenate([hi, lo], axis=0), fp[c])
        o = o[:160] + o[160:]
        for h in range(2):
            cols = o[:, 128 * h : 128 * h + 128]
            part = cols[:128].reshape(8, 2, 8, 128)
            for a2_ in range(2):
                ptl[at, :, 2 * a2_ + h] = part[:, a2_]
            for p in range(8):
                ptl[at, p, 4, pl.ds(4 * h, 4), :] = cols[128 + 4 * p : 132 + 4 * p]

    valid_features(k, 1)
    forwarded(zfv, s_fwv, r_fwv)
    valid_features(other, 0)
    tw_v = remote(pvl.at[0], pvtw, s_tw.at[1], r_tw.at[1], twin)
    tw_v.start()
    tw_v.wait_recv()
    pvl[1] = pvl[1] + pvtw[...]
    b_v = to_chips(lambda to: pvl.at[1, to], lambda i: bvr.at[i], s_bv, r_bv)
    a2t += forward(zft, s_a2t, r_a2t, s_fwt, r_fwt)
    forwarded(zft, s_fwt, r_fwt)
    for i in range(5):
        train_pair(other, i)
    train_features(other, 0)
    tw_t = remote(ptl.at[0], pttw, s_tw.at[2], r_tw.at[2], twin)
    tw_t.start()
    for i in range(5):
        train_pair(k, i)
    train_features(k, 1)
    tw_t.wait_recv()
    ptl[1] = ptl[1] + pttw[...]
    b_t = to_chips(lambda to: ptl.at[1, to], lambda i: btr.at[i], s_bt, r_bt)

    par = lax.rem(zm, 2)
    slot = lax.div(zm, 2) * 2 + zr
    mine = zr == par
    c_v = []
    for j in PAIR_OFFSETS:
        peer = (dp_at(y, 2 * lax.rem(zm + j, 8) + par), f)
        c_v.append(remote(vs, vg.at[slot], s_c.at[j], r_c.at[slot], peer))
    keep_v = pltpu.make_async_copy(vs, vg.at[slot], r_c.at[slot])

    pl.semaphore_wait(tok.at[2], 2)
    vs[...] = summed(pvl[1, q], b_v, bvr)
    for cp in c_v[:7]:
        cp.start()

    @pl.when(mine)
    def _():
        keep_v.start()

    @pl.when(jnp.logical_not(mine))
    def _():
        c_v[7].start()

    total = summed(ptl[1, q], b_t, btr)
    ts[...] = total
    blk = 2 * y + zr
    tg[blk] = total
    partners = (
        (1 - y, zo, 2 * (1 - y) + 1 - zr),
        (1 - y, z, 2 * (1 - y) + zr),
        (y, zo, 2 * y + 1 - zr),
    )
    q_t = [
        remote(ts, tg.at[blk], s_q.at[j], r_q.at[j], (dp_at(py, pz), f))
        for j, (py, pz, _) in enumerate(partners)
    ]
    for cp in q_t:
        cp.start()
    for i in range(8):
        arrived(vs, vg.at[i], r_c.at[i])
    vals = jnp.concatenate([vg[:, t].reshape(64, 128) for t in range(4)], axis=1)
    ones = jnp.ones((8, HALF), F32)
    nv = dot_nt(ones, vals * vals, lax.Precision.HIGHEST)
    for j, (_, _, pb) in enumerate(partners):
        remote(ts, tg.at[pb], s_q.at[j], r_q.at[j], twin).wait_recv()

    tail = tg[:, 4].reshape(32, 128)
    row = iota((32, 128), 0) & 7
    quarter = 2 * (lax.shift_right_logical(row, 1) & 1) + lax.shift_right_logical(row, 2)
    lhs = []
    na = jnp.zeros((32, 1), F32)
    for t in range(4):
        top = tg[:, t].reshape(32, 128)
        na = na + jnp.sum(top * top, axis=1, keepdims=True)
        lhs.append(jnp.concatenate([top, jnp.where(quarter == t, tail, 0.0)], axis=0))
    nb = jnp.sum(tail * tail, axis=1, keepdims=True)
    cos = dot_nt(jnp.concatenate(lhs, axis=1), vals, lax.Precision.HIGHEST)
    nv4 = jnp.concatenate([nv] * 4, axis=0)
    half32 = lambda n: jnp.broadcast_to(n, (32, 32))
    msg_a = jnp.concatenate([cos[:32], nv4], axis=1)
    msg_b = jnp.concatenate([cos[32:], half32(na), half32(nb)], axis=1)
    ds[:, 0] = msg_a.reshape(4, 8, 128)
    ds[:, 1] = msg_b.reshape(4, 8, 128)
    d_c = []
    for by in range(2):
        for br in range(2):
            for i in range(4):
                to_f = 8 * y + 2 * i + zr
                b = 2 * by + br
                j = 4 * b + i
                here = jnp.logical_and(jnp.logical_and(y == by, zr == br), f == to_f)
                cp = remote(
                    ds.at[b], dr.at[f], s_d.at[j], r_d.at[f], (dp_at(by, 2 * zm + br), to_f)
                )
                keep = pltpu.make_async_copy(ds.at[b], dr.at[f], r_d.at[f])
                d_c.append((cp, here))

                @pl.when(jnp.logical_not(here))
                def _():
                    cp.start()

                @pl.when(here)
                def _():
                    keep.start()

    for cp in [tw_av, tw_at, tw_v, tw_t] + a1v + a1t + a2v + a2t + b_v + b_t + c_v[:7] + q_t:
        cp.wait_send()

    @pl.when(jnp.logical_not(mine))
    def _():
        c_v[7].wait_send()

    for i in range(16):
        arrived(ds.at[0], dr.at[i], r_d.at[i])
    sa = dr[0, 0]
    sb = dr[0, 1]
    for i in range(1, 16):
        sa = sa + dr[i, 0]
        sb = sb + dr[i, 1]
    inv_v = lax.rsqrt(sa[:, 64:128] + NORM_EPS)
    res_a = sa[:, 0:64] * lax.rsqrt(sb[:, 64:65] + NORM_EPS) * inv_v
    s2 = (sb[0:2] + sb[2:4]) + (sb[4:6] + sb[6:8])
    res_b = s2[:, 0:64] * lax.rsqrt(s2[:, 96:97] + NORM_EPS) * inv_v[0:2]
    pick = lax.rem(lax.div(f, 2), 4)
    for res, rows in ((res_a, pl.ds(0, 8)), (res_b, pl.ds(8, 2))):
        o = res[:, 0:16]
        for i in range(1, 4):
            o = jnp.where(pick == i, res[:, 16 * i : 16 * i + 16], o)
        out[rows, :] = o
    for cp, here in d_c:

        @pl.when(jnp.logical_not(here))
        def _():
            cp.wait_send()


def body(xt, ct, lt, xv, cv, lv, ad, au, mom1, mom2, rank_p, feat_p):
    dma = pltpu.SemaphoreType.DMA
    tile = lambda *lead: pltpu.VMEM(lead + (8, 128), F32)
    scratch = [
        pltpu.VMEM((2, NT + NV, HALF), BF16),
        pltpu.VMEM((2, 64, HALF), BF16),
        pltpu.VMEM((2, 16, 64), BF16),
        pltpu.VMEM((2, HALF, 256), BF16),
        pltpu.VMEM((2, 64, HALF), F32),
        pltpu.VMEM((2, 64, HALF), F32),
        pltpu.VMEM((10, SEG), jnp.int32),
        pltpu.VMEM((8, SEG), jnp.int32),
        tile(2, 8, 2),
        tile(8, 2),
        tile(7, 2),
        tile(2, 8, 2),
        tile(2, 8, 7),
        tile(8, 7),
        tile(7, 7),
        tile(2, 8, 7),
        pltpu.VMEM((16, 1024), F32),
        pltpu.VMEM((8, 1024), F32),
        pltpu.VMEM((2, 128, HALF), BF16),
        pltpu.VMEM((2, 32, 128), BF16),
        pltpu.VMEM((640, HALF), BF16),
        tile(2, 8, 4),
        tile(8, 4),
        tile(7, 4),
        tile(2, 8, 5),
        tile(8, 5),
        tile(7, 5),
        tile(4),
        tile(5),
        tile(8, 4),
        tile(4, 5),
        tile(4, 2),
        tile(16, 2),
        dma((8,)),
        dma((2, 3)),
        dma((4,)), dma((4,)),
        dma((7,)), dma((7,)),
        dma((7,)), dma((7,)),
        dma((8,)), dma((8,)),
        dma((7,)), dma((7,)),
        dma((7,)), dma((7,)),
        dma((8,)), dma((8,)),
        dma((7,)), dma((7,)),
        dma((7,)), dma((7,)),
        dma((8,)), dma((8,)),
        dma((3,)), dma((3,)),
        dma((16,)), dma((16,)),
        pltpu.SemaphoreType.REGULAR((3,)),
    ]
    return pl.pallas_call(
        kernel,
        name="features",
        out_shape=jax.ShapeDtypeStruct((10, 16), F32),
        in_specs=[pl.BlockSpec(memory_space=pltpu.HBM)] * 12,
        out_specs=pl.BlockSpec(memory_space=pltpu.VMEM),
        scratch_shapes=scratch,
        compiler_params=pltpu.CompilerParams(
            collective_id=0, has_side_effects=True, vmem_limit_bytes=60 << 20
        ),
    )(
        xt.reshape(NT, HALF), ct.reshape(NT, HALF), lt,
        xv.reshape(NV, HALF), cv.reshape(NV, HALF), lv,
        ad, au, mom1, mom2, jnp.swapaxes(rank_p, 1, 2), feat_p,
    )


def solution(mesh):
    placed = (
        P("dp", None, "fsdp"),
        P("dp", None, "fsdp"),
        P("dp", None),
        P("dp", None, "fsdp"),
        P("dp", None, "fsdp"),
        P("dp", None),
        P(None, "fsdp"),
        P(None, "fsdp"),
        P(None, None, "fsdp"),
        P(None, None, "fsdp"),
        P(),
        P(None, "fsdp", None),
    )
    return jax.shard_map(
        body, mesh=mesh, in_specs=placed, out_specs=P("dp", "fsdp"), check_vma=False
    )
```

```python
import jax
import jax.numpy as jnp
from jax import lax
from jax.experimental import pallas as pl
from jax.experimental.pallas import tpu as pltpu
from jax.sharding import PartitionSpec as P

ADAPTER_SCALE = 2.0
BETA_FIRST = 0.9
BETA_SECOND = 0.999
ADAM_EPS = 1e-08
NORM_EPS = 1e-06

MESH = pl.DeviceIdType.MESH
F32 = jnp.float32
BF16 = jnp.bfloat16
SEG = 96
NT = 960
NV = 768
HALF = 512

OFFSETS = ((2, 1), (1, 1), (3, 1), (2, 0), (0, 1), (1, 0), (3, 0))
PAIR_OFFSETS = (4, 3, 5, 2, 6, 1, 7, 0)


def dot(a, b):
    return lax.dot_general(a, b, (((1,), (0,)), ((), ())), preferred_element_type=F32)


def dot_nt(a, b, precision=None):
    return lax.dot_general(
        a, b, (((1,), (1,)), ((), ())), preferred_element_type=F32, precision=precision
    )


def split(x):
    hi = x.astype(BF16)
    return hi, (x - hi.astype(F32)).astype(BF16)


def kernel(
    xt, ct, lt, xv, cv, lv, ad, au, mom1, mom2, rank_p, feat_p,
    out,
    buf, w, rp, fp, m_, v_, labt, labv,
    zv, zvtw, arv, zfv, zt, zttw, art, zft, wt, bd, pm8, pm2, dirs,
    pvl, pvtw, bvr, ptl, pttw, btr, vs, ts, vg, tg, ds, dr,
    ld, la, s_tw, r_tw, s_a1v, r_a1v, s_a2v, r_a2v, s_fwv, r_fwv,
    s_a1t, r_a1t, s_a2t, r_a2t, s_fwt, r_fwt, s_bv, r_bv, s_bt, r_bt,
    s_c, r_c, s_q, r_q, s_d, r_d, tok,
):
    d = lax.axis_index("dp")
    f = lax.axis_index("fsdp")
    y, z = lax.div(d, 16), lax.rem(d, 16)
    zm, zr = lax.div(z, 2), lax.rem(z, 2)
    q, k = lax.div(f, 2), lax.rem(f, 2)
    x, yh = lax.div(q, 2), lax.rem(q, 2)
    other = 1 - k
    twin = (d, f + 1 - 2 * k)
    chips = []
    for dx, dy in OFFSETS:
        to = lax.rem(x + dx, 4) * 2 + lax.rem(yh + dy, 2)
        fro = lax.rem(x + 4 - dx, 4) * 2 + lax.rem(yh + dy, 2)
        chips.append((to, fro))

    def dp_at(y_at, z_at):
        return y_at * 16 + z_at

    def z_off(n):
        return dp_at(y, lax.rem(z + n + 16, 16))

    barrier = pltpu.get_barrier_semaphore()
    zo = z + 1 - 2 * zr
    greet = [(d, to * 2 + k) for to, _ in chips]
    greet += [twin, (dp_at(1 - y, z), f), (dp_at(y, zo), f), (dp_at(1 - y, zo), f)]
    greet += [(dp_at(y, lax.rem(z + 15 + 2 * zr, 16)), f)]
    for peer in greet:
        pl.semaphore_signal(barrier, inc=1, device_id=peer, device_id_type=MESH)

    last = 896
    loads = (
        (au, w.at[0]),
        (ad, w.at[1]),
        (rank_p, rp),
        (lt, labt),
        (lv, labv),
        (feat_p, fp),
        (mom1, m_),
        (mom2, v_),
    )
    load = [pltpu.make_async_copy(a, b, ld.at[i]) for i, (a, b) in enumerate(loads)]
    acts = []
    for c, (tr, va) in enumerate(((ct, cv), (xt, xv))):
        acts.append(
            [
                pltpu.make_async_copy(a, buf.at[c, pl.ds(to, n)], la.at[c, i])
                for i, (a, to, n) in enumerate(
                    (
                        (va, NT, NV),
                        (tr.at[pl.ds(last, NT - last)], last, NT - last),
                        (tr.at[pl.ds(0, last)], 0, last),
                    )
                )
            ]
        )
    for cp in load[:3]:
        cp.start()
    for mine_k in range(2):

        @pl.when(k == mine_k)
        def _():
            for i in (0, 1, 2):
                for c in (1 - mine_k, mine_k):
                    acts[c][i].start()

    for cp in load[3:]:
        cp.start()

    def loaded(c, i):
        src = xt.at[pl.ds(0, (NV, NT - last, last)[i])] if i else xv
        at = (NT, last, 0)[i]
        pltpu.make_async_copy(
            src, buf.at[c, pl.ds(at, (NV, NT - last, last)[i])], la.at[c, i]
        ).wait()

    def remote(src, dst, send, recv, peer):
        return pltpu.make_async_remote_copy(
            src_ref=src, dst_ref=dst, send_sem=send, recv_sem=recv,
            device_id=peer, device_id_type=MESH,
        )

    def arrived(src, dst, sem):
        pltpu.make_async_copy(src, dst, sem).wait()

    lane = lax.broadcasted_iota(jnp.int32, (16, 128), 1)

    def inner_valid(c, at):
        wc = w[c]
        hi, lo = split(dot(rp[c], wc))
        both = jnp.concatenate([hi, lo], axis=0)
        tail = dot_nt(wc, buf[c, pl.ds(last, 128), :])
        for g in range(4):
            rows = jnp.concatenate(
                [
                    buf[c, pl.ds(NT + 192 * g, 128), :],
                    buf[c, pl.ds(NT + 192 * g + 64, 128), :],
                ],
                axis=0,
            )
            o = dot_nt(both, rows)
            o = o[:16] + o[16:]
            zv[at, 2 * g : 2 * g + 2, 1] = o[:, :128].reshape(2, 8, 128)
            mixed = jnp.where(lane < 64, tail[16 * g : 16 * g + 16], o[:, 128:])
            zv[at, 2 * g : 2 * g + 2, 0] = mixed.reshape(2, 8, 128)

    def inner_train(c, at):
        wc = w[c]
        for t in range(4):
            n = 256 if t < 3 else 128
            o = dot_nt(wc, buf[c, pl.ds(256 * t, n), :])
            for j in range(n // 128):
                zt[at, :, 2 * t + j] = o[:, 128 * j : 128 * j + 128].reshape(8, 8, 128)

    def to_chips(src, dst, send, recv):
        cps = [
            remote(src(to), dst(i), send.at[i], recv.at[i], (d, to * 2 + k))
            for i, (to, _) in enumerate(chips)
        ]
        for cp in cps:
            cp.start()
        return cps

    for i in range(3):
        load[i].wait()
    for c in (other, k):
        loaded(c, 0)
        loaded(c, 1)
        inner_valid(c, 0) if c is other else inner_valid(c, 1)
        if c is other:
            pl.semaphore_wait(barrier, len(greet))
            tw_av = remote(zv.at[0], zvtw, s_tw.at[0], r_tw.at[0], twin)
            tw_av.start()
            for n in (-1, 1):
                pl.semaphore_signal(
                    tok.at[0], inc=1, device_id=(z_off(n), f), device_id_type=MESH
                )
    tw_av.wait_recv()
    zv[1] = zv[1] + zvtw[...]
    a1v = to_chips(lambda to: zv.at[1, to], lambda i: arv.at[i], s_a1v, r_a1v)
    loaded(other, 2)
    inner_train(other, 0)
    tw_at = remote(zt.at[0], zttw, s_tw.at[3], r_tw.at[3], twin)
    tw_at.start()
    loaded(k, 2)
    inner_train(k, 1)
    tw_at.wait_recv()
    zt[1] = zt[1] + zttw[...]
    a1t = to_chips(lambda to: zt.at[1, to], lambda i: art.at[i], s_a1t, r_a1t)

    for cp in load[3:]:
        cp.wait()
    iota = lambda shape, dim: lax.broadcasted_iota(jnp.int32, shape, dim)
    one = lambda cond: jnp.where(cond, 1.0, 0.0)
    tl = iota((1, 1024), 1)
    seg = jnp.zeros((1, 1024), jnp.int32)
    for j in range(1, 11):
        seg = seg + jnp.where(tl >= SEG * j, 1, 0)
    kept = one(labt[...] != -100)
    scale = ADAPTER_SCALE / jnp.sum(kept, axis=1, keepdims=True)
    spread = one(iota((SEG, 1024), 0) == tl - SEG * seg).astype(BF16)
    laid = dot(kept.astype(BF16), spread)
    wt[0:10, :] = jnp.where(iota((10, 1024), 0) == seg, laid * scale, 0.0)
    grp = lax.shift_right_logical(tl, 8)
    u = tl - 256 * grp
    tokv = jnp.where(u < 128, u, u - 64)
    valid = jnp.where(u < 128, 1, jnp.where(u >= 192, 1, 0))
    late = jnp.where(tokv >= SEG, 1, 0)
    segv = jnp.where(valid > 0, 2 * grp + late, -1)
    keptv = one(labv[...] != -100)
    spread = one(iota((SEG, 1024), 0) == tokv - SEG * late).astype(BF16)
    bd[...] = jnp.where(iota((8, 1024), 0) == segv, dot(keptv.astype(BF16), spread), 0.0)
    up8 = one(lax.shift_right_logical(iota((128, 16), 0), 3) == iota((128, 16), 1)).astype(BF16)
    up2 = one(lax.shift_right_logical(iota((32, 16), 0), 1) == iota((32, 16), 1)).astype(BF16)
    wide = one((iota((64, HALF), 1) & 63) == iota((64, HALF), 0)).astype(BF16)
    in8 = (iota((128, HALF), 0) & 7) == lax.shift_right_logical(iota((128, HALF), 1), 6)
    in2 = (iota((32, 128), 0) & 1) == lax.shift_right_logical(iota((32, 128), 1), 6)
    for c in range(2):
        pc = rp[c]
        a8 = dot(dot(up8, pc).astype(BF16), wide)
        pm8[c] = jnp.where(in8, a8, 0.0).astype(BF16)
        a2 = dot(dot(up2, pc).astype(BF16), wide[:, :128])
        pm2[c] = jnp.where(in2, a2, 0.0).astype(BF16)

    pl.semaphore_wait(tok.at[0], 2)
    for n in (-2, 2):
        pl.semaphore_signal(tok.at[1], inc=1, device_id=(z_off(n), f), device_id_type=MESH)

    def summed(own, cps, parts):
        total = own
        for i in reversed(range(7)):
            cps[i].wait_recv()
            total = total + parts[i]
        return total

    def spread_out(zf, send, recv, fsend, frecv):
        cps = to_chips(lambda to: zf.at[k, q], lambda i: zf.at[k, q], send, recv)
        cp = remote(zf.at[k, q], zf.at[k, q], fsend.at[7], frecv.at[7], twin)
        cp.start()
        return cps + [cp]

    def forward(zf, send, recv, fsend, frecv):
        cps = []
        for i in reversed(range(7)):
            fro = chips[i][1]
            at = zf.at[k, fro]
            remote(at, at, send.at[i], recv.at[i], twin).wait_recv()
            cps.append(remote(at, at, fsend.at[i], frecv.at[i], twin))
            cps[-1].start()
        return cps

    def forwarded(zf, fsend, frecv):
        for i in range(8):
            at = zf.at[other, q if i == 7 else chips[i][1]]
            remote(at, at, fsend.at[i], frecv.at[i], twin).wait_recv()

    zfv[k, q] = summed(zv[1, q], a1v, arv)
    a2v = spread_out(zfv, s_a2v, r_a2v, s_fwv, r_fwv)
    zft[k, q] = summed(zt[1, q], a1t, art)
    a2t = spread_out(zft, s_a2t, r_a2t, s_fwt, r_fwt)
    pl.semaphore_wait(tok.at[1], 2)
    for n in (-4, 4):
        pl.semaphore_signal(tok.at[2], inc=1, device_id=(z_off(n), f), device_id_type=MESH)
    a2v += forward(zfv, s_a2v, r_a2v, s_fwv, r_fwv)

    def valid_features(c, at):
        lhs, rhs = [], []
        for g in range(4):
            za = zfv[c, 2 * g : 2 * g + 2, 1].reshape(16, 128)
            zb = zfv[c, 2 * g : 2 * g + 2, 0].reshape(16, 128)
            zg = jnp.concatenate([za, zb], axis=1)
            hi = zg.astype(BF16).astype(F32)
            lo = zg - hi
            mask = bd[:, 256 * g : 256 * g + 256]
            blocks = [
                jnp.broadcast_to(part[a : a + 1], (8, 256)) * mask
                for part in (hi, lo)
                for a in range(16)
            ]
            lhs.append(jnp.concatenate(blocks, axis=0).astype(BF16))
        left = []
        for n in range(2):
            cols = pl.ds(256 * n, 256)
            acc = None
            for g in range(4):
                rows = jnp.concatenate(
                    [
                        buf[1 - c, pl.ds(NT + 192 * g, 128), cols],
                        buf[1 - c, pl.ds(NT + 192 * g + 64, 128), cols],
                    ],
                    axis=0,
                )
                o = dot(lhs[g], rows)
                acc = o if acc is None else acc + o
            left.append(acc[:128] + acc[128:])
        hi, lo = split(jnp.concatenate(left, axis=1))
        o = dot(jnp.concatenate([hi, lo], axis=0), fp[c])
        o = o[:128] + o[128:]
        for h in range(2):
            part = o[:, 128 * h : 128 * h + 128].reshape(8, 2, 8, 128)
            for a2_ in range(2):
                pvl[at, :, 2 * a2_ + h] = part[:, a2_]

    def train_pair(c, i):
        t0 = (192 * i) // 128
        second = zft[c, :, t0 + 1] if t0 < 6 else zfv[c, :, 0]
        zg = jnp.concatenate([zft[c, :, t0].reshape(64, 128), second.reshape(64, 128)], axis=1)
        cols = pl.ds(128 * t0, 256)
        lhs = jnp.concatenate(
            [zg * wt[2 * i : 2 * i + 1, cols], zg * wt[2 * i + 1 : 2 * i + 2, cols]], axis=0
        ).astype(BF16)
        for n in range(2):
            at = pl.ds(256 * n, 256)
            g2 = dot(lhs, buf[1 - c, pl.ds(128 * t0, 256), at])
            m = BETA_FIRST * m_[c, :, at]
            v = BETA_SECOND * v_[c, :, at]
            for s in range(2):
                g = g2[64 * s : 64 * s + 64]
                num = m + (1.0 - BETA_FIRST) * g
                second = v + (1.0 - BETA_SECOND) * g * g
                den = second * lax.rsqrt(second) + ADAM_EPS
                dirs[pl.ds(128 * i + 64 * s, 64), at] = (num / den).astype(BF16)

    def train_features(c, at):
        l8 = dot(pm8[c], dirs[pl.ds(0, 512), :])
        l2 = dot(pm2[c], dirs[pl.ds(512, 128), :])
        hi, lo = split(jnp.concatenate([l8, l2], axis=0))
        o = dot(jnp.concatenate([hi, lo], axis=0), fp[c])
        o = o[:160] + o[160:]
        for h in range(2):
            cols = o[:, 128 * h : 128 * h + 128]
            part = cols[:128].reshape(8, 2, 8, 128)
            for a2_ in range(2):
                ptl[at, :, 2 * a2_ + h] = part[:, a2_]
            for p in range(8):
                ptl[at, p, 4, pl.ds(4 * h, 4), :] = cols[128 + 4 * p : 132 + 4 * p]

    valid_features(k, 1)
    forwarded(zfv, s_fwv, r_fwv)
    valid_features(other, 0)
    tw_v = remote(pvl.at[0], pvtw, s_tw.at[1], r_tw.at[1], twin)
    tw_v.start()
    tw_v.wait_recv()
    pvl[1] = pvl[1] + pvtw[...]
    b_v = to_chips(lambda to: pvl.at[1, to], lambda i: bvr.at[i], s_bv, r_bv)
    a2t += forward(zft, s_a2t, r_a2t, s_fwt, r_fwt)
    forwarded(zft, s_fwt, r_fwt)
    for i in range(5):
        train_pair(other, i)
    train_features(other, 0)
    tw_t = remote(ptl.at[0], pttw, s_tw.at[2], r_tw.at[2], twin)
    tw_t.start()
    for i in range(5):
        train_pair(k, i)
    train_features(k, 1)
    tw_t.wait_recv()
    ptl[1] = ptl[1] + pttw[...]
    b_t = to_chips(lambda to: ptl.at[1, to], lambda i: btr.at[i], s_bt, r_bt)

    par = lax.rem(zm, 2)
    slot = lax.div(zm, 2) * 2 + zr
    mine = zr == par
    c_v = []
    for j in PAIR_OFFSETS:
        peer = (dp_at(y, 2 * lax.rem(zm + j, 8) + par), f)
        c_v.append(remote(vs, vg.at[slot], s_c.at[j], r_c.at[slot], peer))
    keep_v = pltpu.make_async_copy(vs, vg.at[slot], r_c.at[slot])

    pl.semaphore_wait(tok.at[2], 2)
    vs[...] = summed(pvl[1, q], b_v, bvr)
    for cp in c_v[:7]:
        cp.start()

    @pl.when(mine)
    def _():
        keep_v.start()

    @pl.when(jnp.logical_not(mine))
    def _():
        c_v[7].start()

    total = summed(ptl[1, q], b_t, btr)
    ts[...] = total
    blk = 2 * y + zr
    tg[blk] = total
    partners = (
        (1 - y, zo, 2 * (1 - y) + 1 - zr),
        (1 - y, z, 2 * (1 - y) + zr),
        (y, zo, 2 * y + 1 - zr),
    )
    q_t = [
        remote(ts, tg.at[blk], s_q.at[j], r_q.at[j], (dp_at(py, pz), f))
        for j, (py, pz, _) in enumerate(partners)
    ]
    for cp in q_t:
        cp.start()
    for i in range(8):
        arrived(vs, vg.at[i], r_c.at[i])
    vals = jnp.concatenate([vg[:, t].reshape(64, 128) for t in range(4)], axis=1)
    ones = jnp.ones((8, HALF), F32)
    nv = dot_nt(ones, vals * vals, lax.Precision.HIGHEST)
    for j, (_, _, pb) in enumerate(partners):
        remote(ts, tg.at[pb], s_q.at[j], r_q.at[j], twin).wait_recv()

    tail = tg[:, 4].reshape(32, 128)
    row = iota((32, 128), 0) & 7
    quarter = 2 * (lax.shift_right_logical(row, 1) & 1) + lax.shift_right_logical(row, 2)
    lhs = []
    na = jnp.zeros((32, 1), F32)
    for t in range(4):
        top = tg[:, t].reshape(32, 128)
        na = na + jnp.sum(top * top, axis=1, keepdims=True)
        lhs.append(jnp.concatenate([top, jnp.where(quarter == t, tail, 0.0)], axis=0))
    nb = jnp.sum(tail * tail, axis=1, keepdims=True)
    cos = dot_nt(jnp.concatenate(lhs, axis=1), vals, lax.Precision.HIGHEST)
    nv4 = jnp.concatenate([nv] * 4, axis=0)
    half32 = lambda n: jnp.broadcast_to(n, (32, 32))
    msg_a = jnp.concatenate([cos[:32], nv4], axis=1)
    msg_b = jnp.concatenate([cos[32:], half32(na), half32(nb)], axis=1)
    ds[:, 0] = msg_a.reshape(4, 8, 128)
    ds[:, 1] = msg_b.reshape(4, 8, 128)
    d_c = []
    for by in range(2):
        for br in range(2):
            for i in range(4):
                to_f = 8 * y + 2 * i + zr
                b = 2 * by + br
                j = 4 * b + i
                here = jnp.logical_and(jnp.logical_and(y == by, zr == br), f == to_f)
                cp = remote(
                    ds.at[b], dr.at[f], s_d.at[j], r_d.at[f], (dp_at(by, 2 * zm + br), to_f)
                )
                keep = pltpu.make_async_copy(ds.at[b], dr.at[f], r_d.at[f])
                d_c.append((cp, here))

                @pl.when(jnp.logical_not(here))
                def _():
                    cp.start()

                @pl.when(here)
                def _():
                    keep.start()

    for cp in [tw_av, tw_at, tw_v, tw_t] + a1v + a1t + a2v + a2t + b_v + b_t + c_v[:7] + q_t:
        cp.wait_send()

    @pl.when(jnp.logical_not(mine))
    def _():
        c_v[7].wait_send()

    for cp, here in d_c:

        @pl.when(jnp.logical_not(here))
        def _():
            cp.wait_send()

    for i in range(16):
        arrived(ds.at[0], dr.at[i], r_d.at[i])
    sa = dr[0, 0]
    sb = dr[0, 1]
    for i in range(1, 16):
        sa = sa + dr[i, 0]
        sb = sb + dr[i, 1]
    inv_v = lax.rsqrt(sa[:, 64:128] + NORM_EPS)
    res_a = sa[:, 0:64] * lax.rsqrt(sb[:, 64:65] + NORM_EPS) * inv_v
    s2 = (sb[0:2] + sb[2:4]) + (sb[4:6] + sb[6:8])
    res_b = s2[:, 0:64] * lax.rsqrt(s2[:, 96:97] + NORM_EPS) * inv_v[0:2]
    pick = lax.rem(lax.div(f, 2), 4)
    for res, rows in ((res_a, pl.ds(0, 8)), (res_b, pl.ds(8, 2))):
        o = res[:, 0:16]
        for i in range(1, 4):
            o = jnp.where(pick == i, res[:, 16 * i : 16 * i + 16], o)
        out[rows, :] = o


def body(xt, ct, lt, xv, cv, lv, ad, au, mom1, mom2, rank_p, feat_p):
    dma = pltpu.SemaphoreType.DMA
    tile = lambda *lead: pltpu.VMEM(lead + (8, 128), F32)
    scratch = [
        pltpu.VMEM((2, NT + NV, HALF), BF16),
        pltpu.VMEM((2, 64, HALF), BF16),
        pltpu.VMEM((2, 16, 64), BF16),
        pltpu.VMEM((2, HALF, 256), BF16),
        pltpu.VMEM((2, 64, HALF), F32),
        pltpu.VMEM((2, 64, HALF), F32),
        pltpu.VMEM((10, SEG), jnp.int32),
        pltpu.VMEM((8, SEG), jnp.int32),
        tile(2, 8, 2),
        tile(8, 2),
        tile(7, 2),
        tile(2, 8, 2),
        tile(2, 8, 7),
        tile(8, 7),
        tile(7, 7),
        tile(2, 8, 7),
        pltpu.VMEM((16, 1024), F32),
        pltpu.VMEM((8, 1024), F32),
        pltpu.VMEM((2, 128, HALF), BF16),
        pltpu.VMEM((2, 32, 128), BF16),
        pltpu.VMEM((640, HALF), BF16),
        tile(2, 8, 4),
        tile(8, 4),
        tile(7, 4),
        tile(2, 8, 5),
        tile(8, 5),
        tile(7, 5),
        tile(4),
        tile(5),
        tile(8, 4),
        tile(4, 5),
        tile(4, 2),
        tile(16, 2),
        dma((8,)),
        dma((2, 3)),
        dma((4,)), dma((4,)),
        dma((7,)), dma((7,)),
        dma((7,)), dma((7,)),
        dma((8,)), dma((8,)),
        dma((7,)), dma((7,)),
        dma((7,)), dma((7,)),
        dma((8,)), dma((8,)),
        dma((7,)), dma((7,)),
        dma((7,)), dma((7,)),
        dma((8,)), dma((8,)),
        dma((3,)), dma((3,)),
        dma((16,)), dma((16,)),
        pltpu.SemaphoreType.REGULAR((3,)),
    ]
    return pl.pallas_call(
        kernel,
        name="features",
        out_shape=pltpu.VMEM((10, 16), F32),
        in_specs=[pl.BlockSpec(memory_space=pltpu.HBM)] * 12,
        out_specs=pl.BlockSpec(memory_space=pltpu.VMEM),
        scratch_shapes=scratch,
        compiler_params=pltpu.CompilerParams(
            collective_id=0, has_side_effects=True, vmem_limit_bytes=60 << 20
        ),
    )(
        xt.reshape(NT, HALF), ct.reshape(NT, HALF), lt,
        xv.reshape(NV, HALF), cv.reshape(NV, HALF), lv,
        ad, au, mom1, mom2, jnp.swapaxes(rank_p, 1, 2), feat_p,
    )


def solution(mesh):
    placed = (
        P("dp", None, "fsdp"),
        P("dp", None, "fsdp"),
        P("dp", None),
        P("dp", None, "fsdp"),
        P("dp", None, "fsdp"),
        P("dp", None),
        P(None, "fsdp"),
        P(None, "fsdp"),
        P(None, None, "fsdp"),
        P(None, None, "fsdp"),
        P(),
        P(None, "fsdp", None),
    )
    return jax.shard_map(
        body, mesh=mesh, in_specs=placed, out_specs=P("dp", "fsdp"), check_vma=False
    )
```

```python
import jax
import jax.numpy as jnp
from jax import lax
from jax.experimental import pallas as pl
from jax.experimental.pallas import tpu as pltpu
from jax.sharding import PartitionSpec as P

ADAPTER_SCALE = 2.0
BETA_FIRST = 0.9
BETA_SECOND = 0.999
ADAM_EPS = 1e-08
NORM_EPS = 1e-06

MESH = pl.DeviceIdType.MESH
F32 = jnp.float32
BF16 = jnp.bfloat16
SEG = 96
NT = 960
NV = 768
HALF = 512

OFFSETS = ((2, 1), (1, 1), (3, 1), (2, 0), (0, 1), (1, 0), (3, 0))
PAIR_OFFSETS = (4, 3, 5, 2, 6, 1, 7, 0)


def dot(a, b):
    return lax.dot_general(a, b, (((1,), (0,)), ((), ())), preferred_element_type=F32)


def dot_nt(a, b, precision=None):
    return lax.dot_general(
        a, b, (((1,), (1,)), ((), ())), preferred_element_type=F32, precision=precision
    )


def split(x):
    hi = x.astype(BF16)
    return hi, (x - hi.astype(F32)).astype(BF16)


def kernel(
    xt, ct, lt, xv, cv, lv, ad, au, mom1, mom2, rank_p, feat_p,
    out,
    buf, w, rp, fp, m_, v_, labt, labv,
    zv, zvtw, arv, zfv, zt, zttw, art, zft, wt, bd, pm8, pm2, dirs,
    pvl, pvtw, bvr, ptl, pttw, btr, vs, ts, vg, tg, ds, dr,
    ld, la, s_tw, r_tw, s_a1v, r_a1v, s_a2v, r_a2v, s_fwv, r_fwv,
    s_a1t, r_a1t, s_a2t, r_a2t, s_fwt, r_fwt, s_bv, r_bv, s_bt, r_bt,
    s_c, r_c, s_q, r_q, s_d, r_d, tok,
):
    d = lax.axis_index("dp")
    f = lax.axis_index("fsdp")
    y, z = lax.div(d, 16), lax.rem(d, 16)
    zm, zr = lax.div(z, 2), lax.rem(z, 2)
    q, k = lax.div(f, 2), lax.rem(f, 2)
    x, yh = lax.div(q, 2), lax.rem(q, 2)
    other = 1 - k
    twin = (d, f + 1 - 2 * k)
    chips = []
    for dx, dy in OFFSETS:
        to = lax.rem(x + dx, 4) * 2 + lax.rem(yh + dy, 2)
        fro = lax.rem(x + 4 - dx, 4) * 2 + lax.rem(yh + dy, 2)
        chips.append((to, fro))

    def dp_at(y_at, z_at):
        return y_at * 16 + z_at

    def z_off(n):
        return dp_at(y, lax.rem(z + n + 16, 16))

    barrier = pltpu.get_barrier_semaphore()
    zo = z + 1 - 2 * zr
    greet = [(d, to * 2 + k) for to, _ in chips]
    greet += [twin, (dp_at(1 - y, z), f), (dp_at(y, zo), f), (dp_at(1 - y, zo), f)]
    greet += [(dp_at(y, lax.rem(z + 15 + 2 * zr, 16)), f)]
    for peer in greet:
        pl.semaphore_signal(barrier, inc=1, device_id=peer, device_id_type=MESH)

    last = 896
    loads = (
        (au, w.at[0]),
        (ad, w.at[1]),
        (rank_p, rp),
        (lt, labt),
        (lv, labv),
        (feat_p, fp),
        (mom1, m_),
        (mom2, v_),
    )
    load = [pltpu.make_async_copy(a, b, ld.at[i]) for i, (a, b) in enumerate(loads)]
    acts = []
    for c, (tr, va) in enumerate(((ct, cv), (xt, xv))):
        acts.append(
            [
                pltpu.make_async_copy(a, buf.at[c, pl.ds(to, n)], la.at[c, i])
                for i, (a, to, n) in enumerate(
                    (
                        (va, NT, NV),
                        (tr.at[pl.ds(last, NT - last)], last, NT - last),
                        (tr.at[pl.ds(0, last)], 0, last),
                    )
                )
            ]
        )
    for cp in load[:3]:
        cp.start()
    for mine_k in range(2):

        @pl.when(k == mine_k)
        def _():
            for i in (0, 1, 2):
                for c in (1 - mine_k, mine_k):
                    acts[c][i].start()

    for cp in load[3:]:
        cp.start()

    def loaded(c, i):
        src = xt.at[pl.ds(0, (NV, NT - last, last)[i])] if i else xv
        at = (NT, last, 0)[i]
        pltpu.make_async_copy(
            src, buf.at[c, pl.ds(at, (NV, NT - last, last)[i])], la.at[c, i]
        ).wait()

    def remote(src, dst, send, recv, peer):
        return pltpu.make_async_remote_copy(
            src_ref=src, dst_ref=dst, send_sem=send, recv_sem=recv,
            device_id=peer, device_id_type=MESH,
        )

    def arrived(src, dst, sem):
        pltpu.make_async_copy(src, dst, sem).wait()

    lane = lax.broadcasted_iota(jnp.int32, (16, 128), 1)

    def inner_valid(c, at):
        wc = w[c]
        hi, lo = split(dot(rp[c], wc))
        both = jnp.concatenate([hi, lo], axis=0)
        tail = dot_nt(wc, buf[c, pl.ds(last, 128), :])
        for g in range(4):
            rows = jnp.concatenate(
                [
                    buf[c, pl.ds(NT + 192 * g, 128), :],
                    buf[c, pl.ds(NT + 192 * g + 64, 128), :],
                ],
                axis=0,
            )
            o = dot_nt(both, rows)
            o = o[:16] + o[16:]
            zv[at, 2 * g : 2 * g + 2, 1] = o[:, :128].reshape(2, 8, 128)
            mixed = jnp.where(lane < 64, tail[16 * g : 16 * g + 16], o[:, 128:])
            zv[at, 2 * g : 2 * g + 2, 0] = mixed.reshape(2, 8, 128)

    def inner_train(c, at):
        wc = w[c]
        for t in range(4):
            n = 256 if t < 3 else 128
            o = dot_nt(wc, buf[c, pl.ds(256 * t, n), :])
            for j in range(n // 128):
                zt[at, :, 2 * t + j] = o[:, 128 * j : 128 * j + 128].reshape(8, 8, 128)

    def to_chips(src, dst, send, recv):
        for i, (to, _) in enumerate(chips):
            remote(src(to), dst(i), send, recv, (d, to * 2 + k)).start()

    for i in range(3):
        load[i].wait()
    for c in (other, k):
        loaded(c, 0)
        loaded(c, 1)
        inner_valid(c, 0) if c is other else inner_valid(c, 1)
        if c is other:
            pl.semaphore_wait(barrier, len(greet))
            tw_av = remote(zv.at[0], zvtw, s_tw.at[0], r_tw.at[0], twin)
            tw_av.start()
            for n in (-1, 1):
                pl.semaphore_signal(
                    tok.at[0], inc=1, device_id=(z_off(n), f), device_id_type=MESH
                )
    tw_av.wait_recv()
    zv[1] = zv[1] + zvtw[...]
    to_chips(lambda to: zv.at[1, to], lambda i: arv.at[i], s_a1v, r_a1v)
    loaded(other, 2)
    inner_train(other, 0)
    tw_at = remote(zt.at[0], zttw, s_tw.at[3], r_tw.at[3], twin)
    tw_at.start()
    loaded(k, 2)
    inner_train(k, 1)
    tw_at.wait_recv()
    zt[1] = zt[1] + zttw[...]
    to_chips(lambda to: zt.at[1, to], lambda i: art.at[i], s_a1t, r_a1t)

    for cp in load[3:]:
        cp.wait()
    iota = lambda shape, dim: lax.broadcasted_iota(jnp.int32, shape, dim)
    one = lambda cond: jnp.where(cond, 1.0, 0.0)
    tl = iota((1, 1024), 1)
    seg = jnp.zeros((1, 1024), jnp.int32)
    for j in range(1, 11):
        seg = seg + jnp.where(tl >= SEG * j, 1, 0)
    kept = one(labt[...] != -100)
    scale = ADAPTER_SCALE / jnp.sum(kept, axis=1, keepdims=True)
    spread = one(iota((SEG, 1024), 0) == tl - SEG * seg).astype(BF16)
    laid = dot(kept.astype(BF16), spread)
    wt[0:10, :] = jnp.where(iota((10, 1024), 0) == seg, laid * scale, 0.0)
    grp = lax.shift_right_logical(tl, 8)
    u = tl - 256 * grp
    tokv = jnp.where(u < 128, u, u - 64)
    valid = jnp.where(u < 128, 1, jnp.where(u >= 192, 1, 0))
    late = jnp.where(tokv >= SEG, 1, 0)
    segv = jnp.where(valid > 0, 2 * grp + late, -1)
    keptv = one(labv[...] != -100)
    spread = one(iota((SEG, 1024), 0) == tokv - SEG * late).astype(BF16)
    bd[...] = jnp.where(iota((8, 1024), 0) == segv, dot(keptv.astype(BF16), spread), 0.0)
    up8 = one(lax.shift_right_logical(iota((128, 16), 0), 3) == iota((128, 16), 1)).astype(BF16)
    up2 = one(lax.shift_right_logical(iota((32, 16), 0), 1) == iota((32, 16), 1)).astype(BF16)
    wide = one((iota((64, HALF), 1) & 63) == iota((64, HALF), 0)).astype(BF16)
    in8 = (iota((128, HALF), 0) & 7) == lax.shift_right_logical(iota((128, HALF), 1), 6)
    in2 = (iota((32, 128), 0) & 1) == lax.shift_right_logical(iota((32, 128), 1), 6)
    for c in range(2):
        pc = rp[c]
        a8 = dot(dot(up8, pc).astype(BF16), wide)
        pm8[c] = jnp.where(in8, a8, 0.0).astype(BF16)
        a2 = dot(dot(up2, pc).astype(BF16), wide[:, :128])
        pm2[c] = jnp.where(in2, a2, 0.0).astype(BF16)

    pl.semaphore_wait(tok.at[0], 2)
    for n in (-2, 2):
        pl.semaphore_signal(tok.at[1], inc=1, device_id=(z_off(n), f), device_id_type=MESH)

    def summed(own, parts, recv):
        arrived(parts, parts, recv)
        total = own
        for i in range(7):
            total = total + parts[i]
        return total

    def spread_out(zf, send, recv):
        for i, (dx, _) in enumerate(OFFSETS):
            at = zf.at[k, q]
            remote(at, at, send, recv.at[dx], (d, chips[i][0] * 2 + k)).start()

    def forward(zf, recv, fsend, frecv):
        for dx in (0, 1, 3, 2):
            pair = zf.at[k, pl.ds(2 * lax.rem(x + 4 - dx, 4), 2)]
            come = pair if dx else zf.at[k, pl.ds(2 * x + 1 - yh, 1)]
            arrived(come, come, recv.at[dx])
            remote(pair, pair, fsend, frecv, twin).start()

    def forwarded(zf, frecv):
        arrived(zf.at[other], zf.at[other], frecv)

    zfv[k, q] = summed(zv[1, q], arv, r_a1v)
    spread_out(zfv, s_a2v, r_a2v)
    zft[k, q] = summed(zt[1, q], art, r_a1t)
    spread_out(zft, s_a2t, r_a2t)
    pl.semaphore_wait(tok.at[1], 2)
    for n in (-4, 4):
        pl.semaphore_signal(tok.at[2], inc=1, device_id=(z_off(n), f), device_id_type=MESH)
    forward(zfv, r_a2v, s_fwv, r_fwv)

    def valid_features(c, at):
        lhs, rhs = [], []
        for g in range(4):
            za = zfv[c, 2 * g : 2 * g + 2, 1].reshape(16, 128)
            zb = zfv[c, 2 * g : 2 * g + 2, 0].reshape(16, 128)
            zg = jnp.concatenate([za, zb], axis=1)
            hi = zg.astype(BF16).astype(F32)
            lo = zg - hi
            mask = bd[:, 256 * g : 256 * g + 256]
            blocks = [
                jnp.broadcast_to(part[a : a + 1], (8, 256)) * mask
                for part in (hi, lo)
                for a in range(16)
            ]
            lhs.append(jnp.concatenate(blocks, axis=0).astype(BF16))
        left = []
        for n in range(2):
            cols = pl.ds(256 * n, 256)
            acc = None
            for g in range(4):
                rows = jnp.concatenate(
                    [
                        buf[1 - c, pl.ds(NT + 192 * g, 128), cols],
                        buf[1 - c, pl.ds(NT + 192 * g + 64, 128), cols],
                    ],
                    axis=0,
                )
                o = dot(lhs[g], rows)
                acc = o if acc is None else acc + o
            left.append(acc[:128] + acc[128:])
        hi, lo = split(jnp.concatenate(left, axis=1))
        o = dot(jnp.concatenate([hi, lo], axis=0), fp[c])
        o = o[:128] + o[128:]
        for h in range(2):
            part = o[:, 128 * h : 128 * h + 128].reshape(8, 2, 8, 128)
            for a2_ in range(2):
                pvl[at, :, 2 * a2_ + h] = part[:, a2_]

    def train_pair(c, i):
        t0 = (192 * i) // 128
        second = zft[c, :, t0 + 1] if t0 < 6 else zfv[c, :, 0]
        zg = jnp.concatenate([zft[c, :, t0].reshape(64, 128), second.reshape(64, 128)], axis=1)
        cols = pl.ds(128 * t0, 256)
        lhs = jnp.concatenate(
            [zg * wt[2 * i : 2 * i + 1, cols], zg * wt[2 * i + 1 : 2 * i + 2, cols]], axis=0
        ).astype(BF16)
        for n in range(2):
            at = pl.ds(256 * n, 256)
            g2 = dot(lhs, buf[1 - c, pl.ds(128 * t0, 256), at])
            m = BETA_FIRST * m_[c, :, at]
            v = BETA_SECOND * v_[c, :, at]
            for s in range(2):
                g = g2[64 * s : 64 * s + 64]
                num = m + (1.0 - BETA_FIRST) * g
                second = v + (1.0 - BETA_SECOND) * g * g
                den = second * lax.rsqrt(second) + ADAM_EPS
                dirs[pl.ds(128 * i + 64 * s, 64), at] = (num / den).astype(BF16)

    def train_features(c, at):
        l8 = dot(pm8[c], dirs[pl.ds(0, 512), :])
        l2 = dot(pm2[c], dirs[pl.ds(512, 128), :])
        hi, lo = split(jnp.concatenate([l8, l2], axis=0))
        o = dot(jnp.concatenate([hi, lo], axis=0), fp[c])
        o = o[:160] + o[160:]
        for h in range(2):
            cols = o[:, 128 * h : 128 * h + 128]
            part = cols[:128].reshape(8, 2, 8, 128)
            for a2_ in range(2):
                ptl[at, :, 2 * a2_ + h] = part[:, a2_]
            for p in range(8):
                ptl[at, p, 4, pl.ds(4 * h, 4), :] = cols[128 + 4 * p : 132 + 4 * p]

    valid_features(k, 1)
    forwarded(zfv, r_fwv)
    valid_features(other, 0)
    tw_v = remote(pvl.at[0], pvtw, s_tw.at[1], r_tw.at[1], twin)
    tw_v.start()
    tw_v.wait_recv()
    pvl[1] = pvl[1] + pvtw[...]
    to_chips(lambda to: pvl.at[1, to], lambda i: bvr.at[i], s_bv, r_bv)
    forward(zft, r_a2t, s_fwt, r_fwt)
    forwarded(zft, r_fwt)
    for i in range(5):
        train_pair(other, i)
    train_features(other, 0)
    tw_t = remote(ptl.at[0], pttw, s_tw.at[2], r_tw.at[2], twin)
    tw_t.start()
    for i in range(5):
        train_pair(k, i)
    train_features(k, 1)
    tw_t.wait_recv()
    ptl[1] = ptl[1] + pttw[...]
    to_chips(lambda to: ptl.at[1, to], lambda i: btr.at[i], s_bt, r_bt)

    par = lax.rem(zm, 2)
    slot = lax.div(zm, 2) * 2 + zr
    mine = zr == par
    c_v = []
    for j in PAIR_OFFSETS:
        peer = (dp_at(y, 2 * lax.rem(zm + j, 8) + par), f)
        c_v.append(remote(vs, vg.at[slot], s_c, r_c, peer))
    keep_v = pltpu.make_async_copy(vs, vg.at[slot], r_c)

    pl.semaphore_wait(tok.at[2], 2)
    vs[...] = summed(pvl[1, q], bvr, r_bv)
    for cp in c_v[:7]:
        cp.start()

    @pl.when(mine)
    def _():
        keep_v.start()

    @pl.when(jnp.logical_not(mine))
    def _():
        c_v[7].start()

    total = summed(ptl[1, q], btr, r_bt)
    ts[...] = total
    blk = 2 * y + zr
    tg[blk] = total
    partners = ((1 - y, zo), (1 - y, z), (y, zo))
    q_t = [
        remote(ts, tg.at[blk], s_q, r_q, (dp_at(py, pz), f))
        for py, pz in partners
    ]
    for cp in q_t:
        cp.start()
    arrived(vg, vg, r_c)
    vals = jnp.concatenate([vg[:, t].reshape(64, 128) for t in range(4)], axis=1)
    ones = jnp.ones((8, HALF), F32)
    nv = dot_nt(ones, vals * vals, lax.Precision.HIGHEST)
    three = tg.at[pl.ds(0, 3)]
    arrived(three, three, r_q)

    tail = tg[:, 4].reshape(32, 128)
    row = iota((32, 128), 0) & 7
    quarter = 2 * (lax.shift_right_logical(row, 1) & 1) + lax.shift_right_logical(row, 2)
    lhs = []
    na = jnp.zeros((32, 1), F32)
    for t in range(4):
        top = tg[:, t].reshape(32, 128)
        na = na + jnp.sum(top * top, axis=1, keepdims=True)
        lhs.append(jnp.concatenate([top, jnp.where(quarter == t, tail, 0.0)], axis=0))
    nb = jnp.sum(tail * tail, axis=1, keepdims=True)
    cos = dot_nt(jnp.concatenate(lhs, axis=1), vals, lax.Precision.HIGHEST)
    nv4 = jnp.concatenate([nv] * 4, axis=0)
    half32 = lambda n: jnp.broadcast_to(n, (32, 32))
    msg_a = jnp.concatenate([cos[:32], nv4], axis=1)
    msg_b = jnp.concatenate([cos[32:], half32(na), half32(nb)], axis=1)
    ds[:, 0] = msg_a.reshape(4, 8, 128)
    ds[:, 1] = msg_b.reshape(4, 8, 128)
    for by in range(2):
        for br in range(2):
            for i in range(4):
                to_f = 8 * y + 2 * i + zr
                b = 2 * by + br
                here = jnp.logical_and(jnp.logical_and(y == by, zr == br), f == to_f)
                cp = remote(
                    ds.at[b], dr.at[f], s_d, r_d, (dp_at(by, 2 * zm + br), to_f)
                )
                keep = pltpu.make_async_copy(ds.at[b], dr.at[f], r_d)

                @pl.when(jnp.logical_not(here))
                def _():
                    cp.start()

                @pl.when(here)
                def _():
                    keep.start()

    for cp in (tw_av, tw_at, tw_v, tw_t):
        cp.wait_send()
    for ref, sem in (
        (arv, s_a1v), (art, s_a1t), (arv, s_a2v), (art, s_a2t), (zfv.at[0], s_fwv),
        (zft.at[0], s_fwt), (bvr, s_bv), (btr, s_bt), (three, s_q),
    ):
        arrived(ref, ref, sem)
    listed = jnp.logical_and(lax.div(f, 8) == y, lax.rem(f, 2) == zr)
    for cond, full, sem in ((mine, vg, s_c), (listed, dr, s_d)):
        most = full.at[pl.ds(0, full.shape[0] - 1)]

        @pl.when(cond)
        def _():
            arrived(most, most, sem)

        @pl.when(jnp.logical_not(cond))
        def _():
            arrived(full, full, sem)

    arrived(dr, dr, r_d)
    sa = dr[0, 0]
    sb = dr[0, 1]
    for i in range(1, 16):
        sa = sa + dr[i, 0]
        sb = sb + dr[i, 1]
    inv_v = lax.rsqrt(sa[:, 64:128] + NORM_EPS)
    res_a = sa[:, 0:64] * lax.rsqrt(sb[:, 64:65] + NORM_EPS) * inv_v
    s2 = (sb[0:2] + sb[2:4]) + (sb[4:6] + sb[6:8])
    res_b = s2[:, 0:64] * lax.rsqrt(s2[:, 96:97] + NORM_EPS) * inv_v[0:2]
    pick = lax.rem(lax.div(f, 2), 4)
    for res, rows in ((res_a, pl.ds(0, 8)), (res_b, pl.ds(8, 2))):
        o = res[:, 0:16]
        for i in range(1, 4):
            o = jnp.where(pick == i, res[:, 16 * i : 16 * i + 16], o)
        out[rows, :] = o


def body(xt, ct, lt, xv, cv, lv, ad, au, mom1, mom2, rank_p, feat_p):
    dma = pltpu.SemaphoreType.DMA
    tile = lambda *lead: pltpu.VMEM(lead + (8, 128), F32)
    scratch = [
        pltpu.VMEM((2, NT + NV, HALF), BF16),
        pltpu.VMEM((2, 64, HALF), BF16),
        pltpu.VMEM((2, 16, 64), BF16),
        pltpu.VMEM((2, HALF, 256), BF16),
        pltpu.VMEM((2, 64, HALF), F32),
        pltpu.VMEM((2, 64, HALF), F32),
        pltpu.VMEM((10, SEG), jnp.int32),
        pltpu.VMEM((8, SEG), jnp.int32),
        tile(2, 8, 2),
        tile(8, 2),
        tile(7, 2),
        tile(2, 8, 2),
        tile(2, 8, 7),
        tile(8, 7),
        tile(7, 7),
        tile(2, 8, 7),
        pltpu.VMEM((16, 1024), F32),
        pltpu.VMEM((8, 1024), F32),
        pltpu.VMEM((2, 128, HALF), BF16),
        pltpu.VMEM((2, 32, 128), BF16),
        pltpu.VMEM((640, HALF), BF16),
        tile(2, 8, 4),
        tile(8, 4),
        tile(7, 4),
        tile(2, 8, 5),
        tile(8, 5),
        tile(7, 5),
        tile(4),
        tile(5),
        tile(8, 4),
        tile(4, 5),
        tile(4, 2),
        tile(16, 2),
        dma((8,)),
        dma((2, 3)),
        dma((4,)), dma((4,)),
        dma, dma, dma, dma((4,)), dma, dma,
        dma, dma, dma, dma((4,)), dma, dma,
        dma, dma, dma, dma, dma, dma, dma, dma, dma, dma,
        pltpu.SemaphoreType.REGULAR((3,)),
    ]
    return pl.pallas_call(
        kernel,
        name="features",
        out_shape=pltpu.VMEM((10, 16), F32),
        in_specs=[pl.BlockSpec(memory_space=pltpu.HBM)] * 12,
        out_specs=pl.BlockSpec(memory_space=pltpu.VMEM),
        scratch_shapes=scratch,
        compiler_params=pltpu.CompilerParams(
            collective_id=0, has_side_effects=True, vmem_limit_bytes=60 << 20
        ),
    )(
        xt.reshape(NT, HALF), ct.reshape(NT, HALF), lt,
        xv.reshape(NV, HALF), cv.reshape(NV, HALF), lv,
        ad, au, mom1, mom2, jnp.swapaxes(rank_p, 1, 2), feat_p,
    )


def solution(mesh):
    placed = (
        P("dp", None, "fsdp"),
        P("dp", None, "fsdp"),
        P("dp", None),
        P("dp", None, "fsdp"),
        P("dp", None, "fsdp"),
        P("dp", None),
        P(None, "fsdp"),
        P(None, "fsdp"),
        P(None, None, "fsdp"),
        P(None, None, "fsdp"),
        P(),
        P(None, "fsdp", None),
    )
    return jax.shard_map(
        body, mesh=mesh, in_specs=placed, out_specs=P("dp", "fsdp"), check_vma=False
    )
```

```python
import jax
import jax.numpy as jnp
from jax import lax
from jax.experimental import pallas as pl
from jax.experimental.pallas import tpu as pltpu
from jax.sharding import PartitionSpec as P

ADAPTER_SCALE = 2.0
BETA_FIRST = 0.9
BETA_SECOND = 0.999
ADAM_EPS = 1e-08
NORM_EPS = 1e-06

MESH = pl.DeviceIdType.MESH
F32 = jnp.float32
BF16 = jnp.bfloat16
SEG = 96
NT = 960
NV = 768
HALF = 512

OFFSETS = ((2, 1), (1, 1), (3, 1), (2, 0), (0, 1), (1, 0), (3, 0))
PAIR_OFFSETS = (4, 3, 5, 2, 6, 1, 7, 0)


def dot(a, b):
    return lax.dot_general(a, b, (((1,), (0,)), ((), ())), preferred_element_type=F32)


def dot_nt(a, b, precision=None):
    return lax.dot_general(
        a, b, (((1,), (1,)), ((), ())), preferred_element_type=F32, precision=precision
    )


def split(x):
    hi = x.astype(BF16)
    return hi, (x - hi.astype(F32)).astype(BF16)


def kernel(
    xt, ct, lt, xv, cv, lv, ad, au, mom1, mom2, rank_p, feat_p,
    out,
    buf, w, rp, fp, m_, v_, labt, labv,
    zv, zvtw, arv, zfv, zt, zttw, art, zft, wt, bd, pm8, pm2, dirs,
    pvl, pvtw, bvr, ptl, pttw, btr, vs, ts, vg, tg, ds, dr,
    ld, la, s_tw, r_tw, s_a1v, r_a1v, s_a2v, r_a2v, s_fwv, r_fwv,
    s_a1t, r_a1t, s_a2t, r_a2t, s_fwt, r_fwt, s_bv, r_bv, s_bt, r_bt,
    s_c, r_c, s_q, r_q, s_d, r_d, tok,
):
    d = lax.axis_index("dp")
    f = lax.axis_index("fsdp")
    y, z = lax.div(d, 16), lax.rem(d, 16)
    zm, zr = lax.div(z, 2), lax.rem(z, 2)
    q, k = lax.div(f, 2), lax.rem(f, 2)
    x, yh = lax.div(q, 2), lax.rem(q, 2)
    other = 1 - k
    twin = (d, f + 1 - 2 * k)
    chips = []
    for dx, dy in OFFSETS:
        to = lax.rem(x + dx, 4) * 2 + lax.rem(yh + dy, 2)
        fro = lax.rem(x + 4 - dx, 4) * 2 + lax.rem(yh + dy, 2)
        chips.append((to, fro))

    def dp_at(y_at, z_at):
        return y_at * 16 + z_at

    def z_off(n):
        return dp_at(y, lax.rem(z + n + 16, 16))

    barrier = pltpu.get_barrier_semaphore()
    zo = z + 1 - 2 * zr
    greet = [(d, to * 2 + k) for to, _ in chips]
    greet += [twin, (dp_at(1 - y, z), f), (dp_at(y, zo), f), (dp_at(1 - y, zo), f)]
    greet += [(dp_at(y, lax.rem(z + 15 + 2 * zr, 16)), f)]
    for peer in greet:
        pl.semaphore_signal(barrier, inc=1, device_id=peer, device_id_type=MESH)

    last = 896
    loads = (
        (au, w.at[0]),
        (ad, w.at[1]),
        (rank_p, rp),
        (lt, labt),
        (lv, labv),
        (feat_p, fp),
        (mom1, m_),
        (mom2, v_),
    )
    load = [pltpu.make_async_copy(a, b, ld.at[i]) for i, (a, b) in enumerate(loads)]
    acts = []
    for c, (tr, va) in enumerate(((ct, cv), (xt, xv))):
        acts.append(
            [
                pltpu.make_async_copy(a, buf.at[c, pl.ds(to, n)], la.at[c, i])
                for i, (a, to, n) in enumerate(
                    (
                        (va, NT, NV),
                        (tr.at[pl.ds(last, NT - last)], last, NT - last),
                        (tr.at[pl.ds(0, last)], 0, last),
                    )
                )
            ]
        )
    for cp in load[:3]:
        cp.start()
    for mine_k in range(2):

        @pl.when(k == mine_k)
        def _():
            for i in (0, 1, 2):
                for c in (1 - mine_k, mine_k):
                    acts[c][i].start()

    for cp in load[3:]:
        cp.start()

    def loaded(c, i):
        src = xt.at[pl.ds(0, (NV, NT - last, last)[i])] if i else xv
        at = (NT, last, 0)[i]
        pltpu.make_async_copy(
            src, buf.at[c, pl.ds(at, (NV, NT - last, last)[i])], la.at[c, i]
        ).wait()

    def remote(src, dst, send, recv, peer):
        return pltpu.make_async_remote_copy(
            src_ref=src, dst_ref=dst, send_sem=send, recv_sem=recv,
            device_id=peer, device_id_type=MESH,
        )

    def arrived(src, dst, sem):
        pltpu.make_async_copy(src, dst, sem).wait()

    lane = lax.broadcasted_iota(jnp.int32, (16, 128), 1)

    def inner_valid(c, at):
        wc = w[c]
        hi, lo = split(dot(rp[c], wc))
        both = jnp.concatenate([hi, lo], axis=0)
        tail = dot_nt(wc, buf[c, pl.ds(last, 128), :])
        for g in range(4):
            rows = jnp.concatenate(
                [
                    buf[c, pl.ds(NT + 192 * g, 128), :],
                    buf[c, pl.ds(NT + 192 * g + 64, 128), :],
                ],
                axis=0,
            )
            o = dot_nt(both, rows)
            o = o[:16] + o[16:]
            zv[at, 2 * g : 2 * g + 2, 1] = o[:, :128].reshape(2, 8, 128)
            mixed = jnp.where(lane < 64, tail[16 * g : 16 * g + 16], o[:, 128:])
            zv[at, 2 * g : 2 * g + 2, 0] = mixed.reshape(2, 8, 128)

    def inner_train(c, at):
        wc = w[c]
        for t in range(4):
            n = 256 if t < 3 else 128
            o = dot_nt(wc, buf[c, pl.ds(256 * t, n), :])
            for j in range(n // 128):
                zt[at, :, 2 * t + j] = o[:, 128 * j : 128 * j + 128].reshape(8, 8, 128)

    def to_chips(src, dst, send, recv):
        for i, (to, _) in enumerate(chips):
            remote(src(to), dst(i), send, recv, (d, to * 2 + k)).start()

    for i in range(3):
        load[i].wait()
    for c in (other, k):
        loaded(c, 0)
        loaded(c, 1)
        inner_valid(c, 0) if c is other else inner_valid(c, 1)
        if c is other:
            pl.semaphore_wait(barrier, len(greet))
            tw_av = remote(zv.at[0], zvtw, s_tw.at[0], r_tw.at[0], twin)
            tw_av.start()
            for n in (-1, 1):
                pl.semaphore_signal(
                    tok.at[0], inc=1, device_id=(z_off(n), f), device_id_type=MESH
                )
    tw_av.wait_recv()
    zv[1] = zv[1] + zvtw[...]
    to_chips(lambda to: zv.at[1, to], lambda i: arv.at[i], s_a1v, r_a1v)
    loaded(other, 2)
    inner_train(other, 0)
    tw_at = remote(zt.at[0], zttw, s_tw.at[3], r_tw.at[3], twin)
    tw_at.start()
    loaded(k, 2)
    inner_train(k, 1)
    tw_at.wait_recv()
    zt[1] = zt[1] + zttw[...]
    to_chips(lambda to: zt.at[1, to], lambda i: art.at[i], s_a1t, r_a1t)

    for cp in load[3:]:
        cp.wait()
    iota = lambda shape, dim: lax.broadcasted_iota(jnp.int32, shape, dim)
    one = lambda cond: jnp.where(cond, 1.0, 0.0)
    tl = iota((1, 1024), 1)
    seg = jnp.zeros((1, 1024), jnp.int32)
    for j in range(1, 11):
        seg = seg + jnp.where(tl >= SEG * j, 1, 0)
    kept = one(labt[...] != -100)
    scale = ADAPTER_SCALE / jnp.sum(kept, axis=1, keepdims=True)
    spread = one(iota((SEG, 1024), 0) == tl - SEG * seg).astype(BF16)
    laid = dot(kept.astype(BF16), spread)
    wt[0:10, :] = jnp.where(iota((10, 1024), 0) == seg, laid * scale, 0.0)
    grp = lax.shift_right_logical(tl, 8)
    u = tl - 256 * grp
    tokv = jnp.where(u < 128, u, u - 64)
    valid = jnp.where(u < 128, 1, jnp.where(u >= 192, 1, 0))
    late = jnp.where(tokv >= SEG, 1, 0)
    segv = jnp.where(valid > 0, 2 * grp + late, -1)
    keptv = one(labv[...] != -100)
    spread = one(iota((SEG, 1024), 0) == tokv - SEG * late).astype(BF16)
    bd[...] = jnp.where(iota((8, 1024), 0) == segv, dot(keptv.astype(BF16), spread), 0.0)
    up8 = one(lax.shift_right_logical(iota((128, 16), 0), 3) == iota((128, 16), 1)).astype(BF16)
    up2 = one(lax.shift_right_logical(iota((32, 16), 0), 1) == iota((32, 16), 1)).astype(BF16)
    wide = one((iota((64, HALF), 1) & 63) == iota((64, HALF), 0)).astype(BF16)
    in8 = (iota((128, HALF), 0) & 7) == lax.shift_right_logical(iota((128, HALF), 1), 6)
    in2 = (iota((32, 128), 0) & 1) == lax.shift_right_logical(iota((32, 128), 1), 6)
    for c in range(2):
        pc = rp[c]
        a8 = dot(dot(up8, pc).astype(BF16), wide)
        pm8[c] = jnp.where(in8, a8, 0.0).astype(BF16)
        a2 = dot(dot(up2, pc).astype(BF16), wide[:, :128])
        pm2[c] = jnp.where(in2, a2, 0.0).astype(BF16)

    pl.semaphore_wait(tok.at[0], 2)
    for n in (-2, 2):
        pl.semaphore_signal(tok.at[1], inc=1, device_id=(z_off(n), f), device_id_type=MESH)

    def summed(own, parts, recv):
        arrived(parts, parts, recv)
        total = own
        for i in range(7):
            total = total + parts[i]
        return total

    def spread_out(zf, send, recv):
        for i, (dx, _) in enumerate(OFFSETS):
            at = zf.at[k, q]
            remote(at, at, send, recv.at[dx], (d, chips[i][0] * 2 + k)).start()

    def forward(zf, recv, fsend, frecv):
        for dx in (0, 1, 3, 2):
            pair = zf.at[k, pl.ds(2 * lax.rem(x + 4 - dx, 4), 2)]
            come = pair if dx else zf.at[k, pl.ds(2 * x + 1 - yh, 1)]
            arrived(come, come, recv.at[dx])
            remote(pair, pair, fsend, frecv, twin).start()

    def forwarded(zf, frecv):
        arrived(zf.at[other], zf.at[other], frecv)

    zfv[k, q] = summed(zv[1, q], arv, r_a1v)
    spread_out(zfv, s_a2v, r_a2v)
    zft[k, q] = summed(zt[1, q], art, r_a1t)
    spread_out(zft, s_a2t, r_a2t)
    pl.semaphore_wait(tok.at[1], 2)
    for n in (-4, 4):
        pl.semaphore_signal(tok.at[2], inc=1, device_id=(z_off(n), f), device_id_type=MESH)
    forward(zfv, r_a2v, s_fwv, r_fwv)

    def valid_features(c, at):
        lhs, rhs = [], []
        for g in range(4):
            za = zfv[c, 2 * g : 2 * g + 2, 1].reshape(16, 128)
            zb = zfv[c, 2 * g : 2 * g + 2, 0].reshape(16, 128)
            zg = jnp.concatenate([za, zb], axis=1)
            hi = zg.astype(BF16).astype(F32)
            lo = zg - hi
            mask = bd[:, 256 * g : 256 * g + 256]
            blocks = [
                jnp.broadcast_to(part[a : a + 1], (8, 256)) * mask
                for part in (hi, lo)
                for a in range(16)
            ]
            lhs.append(jnp.concatenate(blocks, axis=0).astype(BF16))
        left = []
        for n in range(2):
            cols = pl.ds(256 * n, 256)
            acc = None
            for g in range(4):
                rows = jnp.concatenate(
                    [
                        buf[1 - c, pl.ds(NT + 192 * g, 128), cols],
                        buf[1 - c, pl.ds(NT + 192 * g + 64, 128), cols],
                    ],
                    axis=0,
                )
                o = dot(lhs[g], rows)
                acc = o if acc is None else acc + o
            left.append(acc[:128] + acc[128:])
        hi, lo = split(jnp.concatenate(left, axis=1))
        o = dot(jnp.concatenate([hi, lo], axis=0), fp[c])
        o = o[:128] + o[128:]
        for h in range(2):
            part = o[:, 128 * h : 128 * h + 128].reshape(8, 2, 8, 128)
            for a2_ in range(2):
                pvl[at, :, 2 * a2_ + h] = part[:, a2_]

    def train_pair(c, i, at_dirs):
        t0 = (192 * i) // 128
        second = zft[c, :, t0 + 1] if t0 < 6 else zfv[c, :, 0]
        zg = jnp.concatenate([zft[c, :, t0].reshape(64, 128), second.reshape(64, 128)], axis=1)
        cols = pl.ds(128 * t0, 256)
        lhs = jnp.concatenate(
            [zg * wt[2 * i : 2 * i + 1, cols], zg * wt[2 * i + 1 : 2 * i + 2, cols]], axis=0
        ).astype(BF16)
        for n in range(2):
            at = pl.ds(256 * n, 256)
            g2 = dot(lhs, buf[1 - c, pl.ds(128 * t0, 256), at])
            m = BETA_FIRST * m_[c, :, at]
            v = BETA_SECOND * v_[c, :, at]
            for s in range(2):
                g = g2[64 * s : 64 * s + 64]
                num = m + (1.0 - BETA_FIRST) * g
                second = v + (1.0 - BETA_SECOND) * g * g
                den = second * lax.rsqrt(second) + ADAM_EPS
                dirs[at_dirs, pl.ds(128 * i + 64 * s, 64), at] = (num / den).astype(BF16)

    def train_features(c, at):
        l8 = dot(pm8[c], dirs[at, pl.ds(0, 512), :])
        l2 = dot(pm2[c], dirs[at, pl.ds(512, 128), :])
        hi, lo = split(jnp.concatenate([l8, l2], axis=0))
        o = dot(jnp.concatenate([hi, lo], axis=0), fp[c])
        o = o[:160] + o[160:]
        for h in range(2):
            cols = o[:, 128 * h : 128 * h + 128]
            part = cols[:128].reshape(8, 2, 8, 128)
            for a2_ in range(2):
                ptl[at, :, 2 * a2_ + h] = part[:, a2_]
            for p in range(8):
                ptl[at, p, 4, pl.ds(4 * h, 4), :] = cols[128 + 4 * p : 132 + 4 * p]

    valid_features(k, 1)
    forwarded(zfv, r_fwv)
    valid_features(other, 0)
    tw_v = remote(pvl.at[0], pvtw, s_tw.at[1], r_tw.at[1], twin)
    tw_v.start()
    tw_v.wait_recv()
    pvl[1] = pvl[1] + pvtw[...]
    to_chips(lambda to: pvl.at[1, to], lambda i: bvr.at[i], s_bv, r_bv)
    forward(zft, r_a2t, s_fwt, r_fwt)
    for i in range(5):
        train_pair(k, i, 1)
    forwarded(zft, r_fwt)
    for i in range(5):
        train_pair(other, i, 0)
    train_features(other, 0)
    tw_t = remote(ptl.at[0], pttw, s_tw.at[2], r_tw.at[2], twin)
    tw_t.start()
    train_features(k, 1)
    par = lax.rem(zm, 2)
    slot = lax.div(zm, 2) * 2 + zr
    mine = zr == par
    c_v = []
    for j in PAIR_OFFSETS:
        peer = (dp_at(y, 2 * lax.rem(zm + j, 8) + par), f)
        c_v.append(remote(vs, vg.at[slot], s_c, r_c, peer))
    keep_v = pltpu.make_async_copy(vs, vg.at[slot], r_c)

    pl.semaphore_wait(tok.at[2], 2)
    vs[...] = summed(pvl[1, q], bvr, r_bv)
    for cp in c_v[:7]:
        cp.start()

    @pl.when(mine)
    def _():
        keep_v.start()

    @pl.when(jnp.logical_not(mine))
    def _():
        c_v[7].start()

    tw_t.wait_recv()
    ptl[1] = ptl[1] + pttw[...]
    to_chips(lambda to: ptl.at[1, to], lambda i: btr.at[i], s_bt, r_bt)

    total = summed(ptl[1, q], btr, r_bt)
    ts[...] = total
    blk = 2 * y + zr
    tg[blk] = total
    partners = ((1 - y, zo), (1 - y, z), (y, zo))
    q_t = [
        remote(ts, tg.at[blk], s_q, r_q, (dp_at(py, pz), f))
        for py, pz in partners
    ]
    for cp in q_t:
        cp.start()
    arrived(vg, vg, r_c)
    vals = jnp.concatenate([vg[:, t].reshape(64, 128) for t in range(4)], axis=1)
    ones = jnp.ones((8, HALF), F32)
    nv = dot_nt(ones, vals * vals, lax.Precision.HIGHEST)
    three = tg.at[pl.ds(0, 3)]
    arrived(three, three, r_q)

    tail = tg[:, 4].reshape(32, 128)
    row = iota((32, 128), 0) & 7
    quarter = 2 * (lax.shift_right_logical(row, 1) & 1) + lax.shift_right_logical(row, 2)
    lhs = []
    na = jnp.zeros((32, 1), F32)
    for t in range(4):
        top = tg[:, t].reshape(32, 128)
        na = na + jnp.sum(top * top, axis=1, keepdims=True)
        lhs.append(jnp.concatenate([top, jnp.where(quarter == t, tail, 0.0)], axis=0))
    nb = jnp.sum(tail * tail, axis=1, keepdims=True)
    cos = dot_nt(jnp.concatenate(lhs, axis=1), vals, lax.Precision.HIGHEST)
    nv4 = jnp.concatenate([nv] * 4, axis=0)
    half32 = lambda n: jnp.broadcast_to(n, (32, 32))
    msg_a = jnp.concatenate([cos[:32], nv4], axis=1)
    msg_b = jnp.concatenate([cos[32:], half32(na), half32(nb)], axis=1)
    ds[:, 0] = msg_a.reshape(4, 8, 128)
    ds[:, 1] = msg_b.reshape(4, 8, 128)
    for by in range(2):
        for br in range(2):
            for i in range(4):
                to_f = 8 * y + 2 * i + zr
                b = 2 * by + br
                here = jnp.logical_and(jnp.logical_and(y == by, zr == br), f == to_f)
                cp = remote(
                    ds.at[b], dr.at[f], s_d, r_d, (dp_at(by, 2 * zm + br), to_f)
                )
                keep = pltpu.make_async_copy(ds.at[b], dr.at[f], r_d)

                @pl.when(jnp.logical_not(here))
                def _():
                    cp.start()

                @pl.when(here)
                def _():
                    keep.start()

    for cp in (tw_av, tw_at, tw_v, tw_t):
        cp.wait_send()
    for ref, sem in (
        (arv, s_a1v), (art, s_a1t), (arv, s_a2v), (art, s_a2t), (zfv.at[0], s_fwv),
        (zft.at[0], s_fwt), (bvr, s_bv), (btr, s_bt), (three, s_q),
    ):
        arrived(ref, ref, sem)
    listed = jnp.logical_and(lax.div(f, 8) == y, lax.rem(f, 2) == zr)
    for cond, full, sem in ((mine, vg, s_c), (listed, dr, s_d)):
        most = full.at[pl.ds(0, full.shape[0] - 1)]

        @pl.when(cond)
        def _():
            arrived(most, most, sem)

        @pl.when(jnp.logical_not(cond))
        def _():
            arrived(full, full, sem)

    arrived(dr, dr, r_d)
    sa = dr[0, 0]
    sb = dr[0, 1]
    for i in range(1, 16):
        sa = sa + dr[i, 0]
        sb = sb + dr[i, 1]
    inv_v = lax.rsqrt(sa[:, 64:128] + NORM_EPS)
    res_a = sa[:, 0:64] * lax.rsqrt(sb[:, 64:65] + NORM_EPS) * inv_v
    s2 = (sb[0:2] + sb[2:4]) + (sb[4:6] + sb[6:8])
    res_b = s2[:, 0:64] * lax.rsqrt(s2[:, 96:97] + NORM_EPS) * inv_v[0:2]
    pick = lax.rem(lax.div(f, 2), 4)
    for res, rows in ((res_a, pl.ds(0, 8)), (res_b, pl.ds(8, 2))):
        o = res[:, 0:16]
        for i in range(1, 4):
            o = jnp.where(pick == i, res[:, 16 * i : 16 * i + 16], o)
        out[rows, :] = o


def body(xt, ct, lt, xv, cv, lv, ad, au, mom1, mom2, rank_p, feat_p):
    dma = pltpu.SemaphoreType.DMA
    tile = lambda *lead: pltpu.VMEM(lead + (8, 128), F32)
    scratch = [
        pltpu.VMEM((2, NT + NV, HALF), BF16),
        pltpu.VMEM((2, 64, HALF), BF16),
        pltpu.VMEM((2, 16, 64), BF16),
        pltpu.VMEM((2, HALF, 256), BF16),
        pltpu.VMEM((2, 64, HALF), F32),
        pltpu.VMEM((2, 64, HALF), F32),
        pltpu.VMEM((10, SEG), jnp.int32),
        pltpu.VMEM((8, SEG), jnp.int32),
        tile(2, 8, 2),
        tile(8, 2),
        tile(7, 2),
        tile(2, 8, 2),
        tile(2, 8, 7),
        tile(8, 7),
        tile(7, 7),
        tile(2, 8, 7),
        pltpu.VMEM((16, 1024), F32),
        pltpu.VMEM((8, 1024), F32),
        pltpu.VMEM((2, 128, HALF), BF16),
        pltpu.VMEM((2, 32, 128), BF16),
        pltpu.VMEM((2, 640, HALF), BF16),
        tile(2, 8, 4),
        tile(8, 4),
        tile(7, 4),
        tile(2, 8, 5),
        tile(8, 5),
        tile(7, 5),
        tile(4),
        tile(5),
        tile(8, 4),
        tile(4, 5),
        tile(4, 2),
        tile(16, 2),
        dma((8,)),
        dma((2, 3)),
        dma((4,)), dma((4,)),
        dma, dma, dma, dma((4,)), dma, dma,
        dma, dma, dma, dma((4,)), dma, dma,
        dma, dma, dma, dma, dma, dma, dma, dma, dma, dma,
        pltpu.SemaphoreType.REGULAR((3,)),
    ]
    return pl.pallas_call(
        kernel,
        name="features",
        out_shape=pltpu.VMEM((10, 16), F32),
        in_specs=[pl.BlockSpec(memory_space=pltpu.HBM)] * 12,
        out_specs=pl.BlockSpec(memory_space=pltpu.VMEM),
        scratch_shapes=scratch,
        compiler_params=pltpu.CompilerParams(
            collective_id=0, has_side_effects=True, vmem_limit_bytes=60 << 20
        ),
    )(
        xt.reshape(NT, HALF), ct.reshape(NT, HALF), lt,
        xv.reshape(NV, HALF), cv.reshape(NV, HALF), lv,
        ad, au, mom1, mom2, jnp.swapaxes(rank_p, 1, 2), feat_p,
    )


def solution(mesh):
    placed = (
        P("dp", None, "fsdp"),
        P("dp", None, "fsdp"),
        P("dp", None),
        P("dp", None, "fsdp"),
        P("dp", None, "fsdp"),
        P("dp", None),
        P(None, "fsdp"),
        P(None, "fsdp"),
        P(None, None, "fsdp"),
        P(None, None, "fsdp"),
        P(),
        P(None, "fsdp", None),
    )
    return jax.shard_map(
        body, mesh=mesh, in_specs=placed, out_specs=P("dp", "fsdp"), check_vma=False
    )
```

```python
import jax
import jax.numpy as jnp
from jax import lax
from jax.experimental import pallas as pl
from jax.experimental.pallas import tpu as pltpu
from jax.sharding import PartitionSpec as P

ADAPTER_SCALE = 2.0
BETA_FIRST = 0.9
BETA_SECOND = 0.999
ADAM_EPS = 1e-08
NORM_EPS = 1e-06

MESH = pl.DeviceIdType.MESH
F32 = jnp.float32
BF16 = jnp.bfloat16
SEG = 96
NT = 960
NV = 768
HALF = 512

OFFSETS = ((2, 1), (1, 1), (3, 1), (2, 0), (0, 1), (1, 0), (3, 0))
PAIR_OFFSETS = (4, 3, 5, 2, 6, 1, 7, 0)


def dot(a, b):
    return lax.dot_general(a, b, (((1,), (0,)), ((), ())), preferred_element_type=F32)


def dot_nt(a, b, precision=None):
    return lax.dot_general(
        a, b, (((1,), (1,)), ((), ())), preferred_element_type=F32, precision=precision
    )


def split(x):
    hi = x.astype(BF16)
    return hi, (x - hi.astype(F32)).astype(BF16)


def kernel(
    xt, ct, lt, xv, cv, lv, ad, au, mom1, mom2, rank_p, feat_p,
    out,
    buf, w, rp, fp, m_, v_, labt, labv,
    zv, zvtw, arv, zfv, zt, zttw, art, zft, wt, bd, pm8, pm2, dirs,
    pvl, pvtw, bvr, ptl, pttw, btr, vs, ts, vg, tg, ds, dr,
    ld, la, s_tw, r_tw, s_a1v, r_a1v, s_a2v, r_a2v, s_fwv, r_fwv,
    s_a1t, r_a1t, s_a2t, r_a2t, s_fwt, r_fwt, s_bv, r_bv, s_bt, r_bt,
    s_c, r_c, s_q, r_q, s_d, r_d, tok,
):
    d = lax.axis_index("dp")
    f = lax.axis_index("fsdp")
    y, z = lax.div(d, 16), lax.rem(d, 16)
    zm, zr = lax.div(z, 2), lax.rem(z, 2)
    q, k = lax.div(f, 2), lax.rem(f, 2)
    x, yh = lax.div(q, 2), lax.rem(q, 2)
    other = 1 - k
    twin = (d, f + 1 - 2 * k)
    chips = []
    for dx, dy in OFFSETS:
        to = lax.rem(x + dx, 4) * 2 + lax.rem(yh + dy, 2)
        fro = lax.rem(x + 4 - dx, 4) * 2 + lax.rem(yh + dy, 2)
        chips.append((to, fro))

    def dp_at(y_at, z_at):
        return y_at * 16 + z_at

    def z_off(n):
        return dp_at(y, lax.rem(z + n + 16, 16))

    barrier = pltpu.get_barrier_semaphore()
    zo = z + 1 - 2 * zr
    greet = [(d, to * 2 + k) for to, _ in chips]
    greet += [twin, (dp_at(1 - y, z), f), (dp_at(y, zo), f), (dp_at(1 - y, zo), f)]
    greet += [(dp_at(y, lax.rem(z + 15 + 2 * zr, 16)), f)]
    for peer in greet:
        pl.semaphore_signal(barrier, inc=1, device_id=peer, device_id_type=MESH)

    last = 896
    loads = (
        (au, w.at[0]),
        (ad, w.at[1]),
        (rank_p, rp),
        (lt, labt),
        (lv, labv),
        (feat_p, fp),
        (mom1, m_),
        (mom2, v_),
    )
    load = [pltpu.make_async_copy(a, b, ld.at[i]) for i, (a, b) in enumerate(loads)]
    acts = []
    for c, (tr, va) in enumerate(((ct, cv), (xt, xv))):
        acts.append(
            [
                pltpu.make_async_copy(a, buf.at[c, pl.ds(to, n)], la.at[c, i])
                for i, (a, to, n) in enumerate(
                    (
                        (va, NT, NV),
                        (tr.at[pl.ds(last, NT - last)], last, NT - last),
                        (tr.at[pl.ds(0, last)], 0, last),
                    )
                )
            ]
        )
    for cp in load[:3]:
        cp.start()
    for mine_k in range(2):

        @pl.when(k == mine_k)
        def _():
            for i in (0, 1, 2):
                for c in (1 - mine_k, mine_k):
                    acts[c][i].start()

    for cp in load[3:]:
        cp.start()

    def loaded(c, i):
        src = xt.at[pl.ds(0, (NV, NT - last, last)[i])] if i else xv
        at = (NT, last, 0)[i]
        pltpu.make_async_copy(
            src, buf.at[c, pl.ds(at, (NV, NT - last, last)[i])], la.at[c, i]
        ).wait()

    def remote(src, dst, send, recv, peer):
        return pltpu.make_async_remote_copy(
            src_ref=src, dst_ref=dst, send_sem=send, recv_sem=recv,
            device_id=peer, device_id_type=MESH,
        )

    def arrived(src, dst, sem):
        pltpu.make_async_copy(src, dst, sem).wait()

    lane = lax.broadcasted_iota(jnp.int32, (16, 128), 1)

    def inner_valid(c, at):
        wc = w[c]
        hi, lo = split(dot(rp[c], wc))
        both = jnp.concatenate([hi, lo], axis=0)
        tail = dot_nt(wc, buf[c, pl.ds(last, 128), :])
        for g in range(4):
            rows = jnp.concatenate(
                [
                    buf[c, pl.ds(NT + 192 * g, 128), :],
                    buf[c, pl.ds(NT + 192 * g + 64, 128), :],
                ],
                axis=0,
            )
            o = dot_nt(both, rows)
            o = o[:16] + o[16:]
            zv[at, 2 * g : 2 * g + 2, 1] = o[:, :128].reshape(2, 8, 128)
            mixed = jnp.where(lane < 64, tail[16 * g : 16 * g + 16], o[:, 128:])
            zv[at, 2 * g : 2 * g + 2, 0] = mixed.reshape(2, 8, 128)

    def inner_train(c, at):
        wc = w[c]
        for t in range(4):
            n = 256 if t < 3 else 128
            o = dot_nt(wc, buf[c, pl.ds(256 * t, n), :])
            for j in range(n // 128):
                zt[at, :, 2 * t + j] = o[:, 128 * j : 128 * j + 128].reshape(8, 8, 128)

    def to_chips(src, dst, send, recv):
        for i, (to, _) in enumerate(chips):
            remote(src(to), dst(i), send, recv, (d, to * 2 + k)).start()

    for i in range(3):
        load[i].wait()
    for c in (other, k):
        loaded(c, 0)
        loaded(c, 1)
        inner_valid(c, 0) if c is other else inner_valid(c, 1)
        if c is other:
            pl.semaphore_wait(barrier, len(greet))
            tw_av = remote(zv.at[0], zvtw, s_tw.at[0], r_tw.at[0], twin)
            tw_av.start()
            for n in (-1, 1):
                pl.semaphore_signal(
                    tok.at[0], inc=1, device_id=(z_off(n), f), device_id_type=MESH
                )
    tw_av.wait_recv()
    zv[1] = zv[1] + zvtw[...]
    to_chips(lambda to: zv.at[1, to], lambda i: arv.at[i], s_a1v, r_a1v)
    loaded(other, 2)
    inner_train(other, 0)
    tw_at = remote(zt.at[0], zttw, s_tw.at[3], r_tw.at[3], twin)
    tw_at.start()
    loaded(k, 2)
    inner_train(k, 1)
    tw_at.wait_recv()
    zt[1] = zt[1] + zttw[...]
    to_chips(lambda to: zt.at[1, to], lambda i: art.at[i], s_a1t, r_a1t)

    for cp in load[3:]:
        cp.wait()
    iota = lambda shape, dim: lax.broadcasted_iota(jnp.int32, shape, dim)
    one = lambda cond: jnp.where(cond, 1.0, 0.0)
    tl = iota((1, 1024), 1)
    seg = jnp.zeros((1, 1024), jnp.int32)
    for j in range(1, 11):
        seg = seg + jnp.where(tl >= SEG * j, 1, 0)
    kept = one(labt[...] != -100)
    scale = ADAPTER_SCALE / jnp.sum(kept, axis=1, keepdims=True)
    spread = one(iota((SEG, 1024), 0) == tl - SEG * seg).astype(BF16)
    laid = dot(kept.astype(BF16), spread)
    wt[0:10, :] = jnp.where(iota((10, 1024), 0) == seg, laid * scale, 0.0)
    grp = lax.shift_right_logical(tl, 8)
    u = tl - 256 * grp
    tokv = jnp.where(u < 128, u, u - 64)
    valid = jnp.where(u < 128, 1, jnp.where(u >= 192, 1, 0))
    late = jnp.where(tokv >= SEG, 1, 0)
    segv = jnp.where(valid > 0, 2 * grp + late, -1)
    keptv = one(labv[...] != -100)
    spread = one(iota((SEG, 1024), 0) == tokv - SEG * late).astype(BF16)
    bd[...] = jnp.where(iota((8, 1024), 0) == segv, dot(keptv.astype(BF16), spread), 0.0)
    up8 = one(lax.shift_right_logical(iota((128, 16), 0), 3) == iota((128, 16), 1)).astype(BF16)
    up2 = one(lax.shift_right_logical(iota((32, 16), 0), 1) == iota((32, 16), 1)).astype(BF16)
    wide = one((iota((64, HALF), 1) & 63) == iota((64, HALF), 0)).astype(BF16)
    in8 = (iota((128, HALF), 0) & 7) == lax.shift_right_logical(iota((128, HALF), 1), 6)
    in2 = (iota((32, 128), 0) & 1) == lax.shift_right_logical(iota((32, 128), 1), 6)
    for c in range(2):
        pc = rp[c]
        a8 = dot(dot(up8, pc).astype(BF16), wide)
        pm8[c] = jnp.where(in8, a8, 0.0).astype(BF16)
        a2 = dot(dot(up2, pc).astype(BF16), wide[:, :128])
        pm2[c] = jnp.where(in2, a2, 0.0).astype(BF16)

    pl.semaphore_wait(tok.at[0], 2)
    for n in (-2, 2):
        pl.semaphore_signal(tok.at[1], inc=1, device_id=(z_off(n), f), device_id_type=MESH)

    def summed(own, parts, recv):
        arrived(parts, parts, recv)
        total = own
        for i in range(7):
            total = total + parts[i]
        return total

    def spread_out(zf, send, recv):
        for i, (dx, _) in enumerate(OFFSETS):
            at = zf.at[k, q]
            remote(at, at, send, recv.at[dx], (d, chips[i][0] * 2 + k)).start()

    def forward(zf, recv, fsend, frecv):
        for dx in (0, 1, 3, 2):
            pair = zf.at[k, pl.ds(2 * lax.rem(x + 4 - dx, 4), 2)]
            come = pair if dx else zf.at[k, pl.ds(2 * x + 1 - yh, 1)]
            arrived(come, come, recv.at[dx])
            remote(pair, pair, fsend, frecv, twin).start()

    def forwarded(zf, frecv):
        arrived(zf.at[other], zf.at[other], frecv)

    zfv[k, q] = summed(zv[1, q], arv, r_a1v)
    spread_out(zfv, s_a2v, r_a2v)
    zft[k, q] = summed(zt[1, q], art, r_a1t)
    spread_out(zft, s_a2t, r_a2t)
    pl.semaphore_wait(tok.at[1], 2)
    for n in (-4, 4):
        pl.semaphore_signal(tok.at[2], inc=1, device_id=(z_off(n), f), device_id_type=MESH)
    for dx in (0, 1, 3, 2):
        at = 2 * x + 1 - yh if dx == 0 else 2 * lax.rem(x + 4 - dx, 4)
        come = zfv.at[k, pl.ds(at, 2 if dx else 1)]
        arrived(come, come, r_a2v.at[dx])
    remote(zfv.at[k], zfv.at[k], s_fwv, r_fwv, twin).start()

    def valid_features(c, at):
        lhs, rhs = [], []
        for g in range(4):
            za = zfv[c, 2 * g : 2 * g + 2, 1].reshape(16, 128)
            zb = zfv[c, 2 * g : 2 * g + 2, 0].reshape(16, 128)
            zg = jnp.concatenate([za, zb], axis=1)
            hi = zg.astype(BF16).astype(F32)
            lo = zg - hi
            mask = bd[:, 256 * g : 256 * g + 256]
            blocks = [
                jnp.broadcast_to(part[a : a + 1], (8, 256)) * mask
                for part in (hi, lo)
                for a in range(16)
            ]
            lhs.append(jnp.concatenate(blocks, axis=0).astype(BF16))
        left = []
        for n in range(2):
            cols = pl.ds(256 * n, 256)
            acc = None
            for g in range(4):
                rows = jnp.concatenate(
                    [
                        buf[1 - c, pl.ds(NT + 192 * g, 128), cols],
                        buf[1 - c, pl.ds(NT + 192 * g + 64, 128), cols],
                    ],
                    axis=0,
                )
                o = dot(lhs[g], rows)
                acc = o if acc is None else acc + o
            left.append(acc[:128] + acc[128:])
        hi, lo = split(jnp.concatenate(left, axis=1))
        o = dot(jnp.concatenate([hi, lo], axis=0), fp[c])
        o = o[:128] + o[128:]
        for h in range(2):
            part = o[:, 128 * h : 128 * h + 128].reshape(8, 2, 8, 128)
            for a2_ in range(2):
                pvl[at, :, 2 * a2_ + h] = part[:, a2_]

    def train_pair(c, i, at_dirs):
        t0 = (192 * i) // 128
        second = zft[c, :, t0 + 1] if t0 < 6 else zfv[c, :, 0]
        zg = jnp.concatenate([zft[c, :, t0].reshape(64, 128), second.reshape(64, 128)], axis=1)
        cols = pl.ds(128 * t0, 256)
        lhs = jnp.concatenate(
            [zg * wt[2 * i : 2 * i + 1, cols], zg * wt[2 * i + 1 : 2 * i + 2, cols]], axis=0
        ).astype(BF16)
        for n in range(2):
            at = pl.ds(256 * n, 256)
            g2 = dot(lhs, buf[1 - c, pl.ds(128 * t0, 256), at])
            m = BETA_FIRST * m_[c, :, at]
            v = BETA_SECOND * v_[c, :, at]
            for s in range(2):
                g = g2[64 * s : 64 * s + 64]
                num = m + (1.0 - BETA_FIRST) * g
                second = v + (1.0 - BETA_SECOND) * g * g
                den = second * lax.rsqrt(second) + ADAM_EPS
                dirs[at_dirs, pl.ds(128 * i + 64 * s, 64), at] = (num / den).astype(BF16)

    def train_features(c, at):
        l8 = dot(pm8[c], dirs[at, pl.ds(0, 512), :])
        l2 = dot(pm2[c], dirs[at, pl.ds(512, 128), :])
        hi, lo = split(jnp.concatenate([l8, l2], axis=0))
        o = dot(jnp.concatenate([hi, lo], axis=0), fp[c])
        o = o[:160] + o[160:]
        for h in range(2):
            cols = o[:, 128 * h : 128 * h + 128]
            part = cols[:128].reshape(8, 2, 8, 128)
            for a2_ in range(2):
                ptl[at, :, 2 * a2_ + h] = part[:, a2_]
            for p in range(8):
                ptl[at, p, 4, pl.ds(4 * h, 4), :] = cols[128 + 4 * p : 132 + 4 * p]

    valid_features(k, 1)
    forwarded(zfv, r_fwv)
    valid_features(other, 0)
    tw_v = remote(pvl.at[0], pvtw, s_tw.at[1], r_tw.at[1], twin)
    tw_v.start()
    tw_v.wait_recv()
    pvl[1] = pvl[1] + pvtw[...]
    to_chips(lambda to: pvl.at[1, to], lambda i: bvr.at[i], s_bv, r_bv)
    forward(zft, r_a2t, s_fwt, r_fwt)
    for i in range(5):
        train_pair(k, i, 1)
    forwarded(zft, r_fwt)
    for i in range(5):
        train_pair(other, i, 0)
    train_features(other, 0)
    tw_t = remote(ptl.at[0], pttw, s_tw.at[2], r_tw.at[2], twin)
    tw_t.start()
    train_features(k, 1)
    par = lax.rem(zm, 2)
    slot = lax.div(zm, 2) * 2 + zr
    mine = zr == par
    c_v = []
    for j in PAIR_OFFSETS:
        peer = (dp_at(y, 2 * lax.rem(zm + j, 8) + par), f)
        c_v.append(remote(vs, vg.at[slot], s_c, r_c, peer))
    keep_v = pltpu.make_async_copy(vs, vg.at[slot], r_c)

    pl.semaphore_wait(tok.at[2], 2)
    vs[...] = summed(pvl[1, q], bvr, r_bv)
    for cp in c_v[:7]:
        cp.start()

    @pl.when(mine)
    def _():
        keep_v.start()

    @pl.when(jnp.logical_not(mine))
    def _():
        c_v[7].start()

    tw_t.wait_recv()
    ptl[1] = ptl[1] + pttw[...]
    to_chips(lambda to: ptl.at[1, to], lambda i: btr.at[i], s_bt, r_bt)

    total = summed(ptl[1, q], btr, r_bt)
    ts[...] = total
    blk = 2 * y + zr
    tg[blk] = total
    partners = ((1 - y, zo), (1 - y, z), (y, zo))
    q_t = [
        remote(ts, tg.at[blk], s_q, r_q, (dp_at(py, pz), f))
        for py, pz in partners
    ]
    for cp in q_t:
        cp.start()
    arrived(vg, vg, r_c)
    vals = jnp.concatenate([vg[:, t].reshape(64, 128) for t in range(4)], axis=1)
    ones = jnp.ones((8, HALF), F32)
    nv = dot_nt(ones, vals * vals, lax.Precision.HIGHEST)
    three = tg.at[pl.ds(0, 3)]
    arrived(three, three, r_q)

    tail = tg[:, 4].reshape(32, 128)
    row = iota((32, 128), 0) & 7
    quarter = 2 * (lax.shift_right_logical(row, 1) & 1) + lax.shift_right_logical(row, 2)
    lhs = []
    na = jnp.zeros((32, 1), F32)
    for t in range(4):
        top = tg[:, t].reshape(32, 128)
        na = na + jnp.sum(top * top, axis=1, keepdims=True)
        lhs.append(jnp.concatenate([top, jnp.where(quarter == t, tail, 0.0)], axis=0))
    nb = jnp.sum(tail * tail, axis=1, keepdims=True)
    cos = dot_nt(jnp.concatenate(lhs, axis=1), vals, lax.Precision.HIGHEST)
    nv4 = jnp.concatenate([nv] * 4, axis=0)
    half32 = lambda n: jnp.broadcast_to(n, (32, 32))
    msg_a = jnp.concatenate([cos[:32], nv4], axis=1)
    msg_b = jnp.concatenate([cos[32:], half32(na), half32(nb)], axis=1)
    ds[:, 0] = msg_a.reshape(4, 8, 128)
    ds[:, 1] = msg_b.reshape(4, 8, 128)
    for by in range(2):
        for br in range(2):
            for i in range(4):
                to_f = 8 * y + 2 * i + zr
                b = 2 * by + br
                here = jnp.logical_and(jnp.logical_and(y == by, zr == br), f == to_f)
                cp = remote(
                    ds.at[b], dr.at[f], s_d, r_d, (dp_at(by, 2 * zm + br), to_f)
                )
                keep = pltpu.make_async_copy(ds.at[b], dr.at[f], r_d)

                @pl.when(jnp.logical_not(here))
                def _():
                    cp.start()

                @pl.when(here)
                def _():
                    keep.start()

    for cp in (tw_av, tw_at, tw_v, tw_t):
        cp.wait_send()
    for ref, sem in (
        (arv, s_a1v), (art, s_a1t), (arv, s_a2v), (art, s_a2t), (zfv.at[0], s_fwv),
        (zft.at[0], s_fwt), (bvr, s_bv), (btr, s_bt), (three, s_q),
    ):
        arrived(ref, ref, sem)
    listed = jnp.logical_and(lax.div(f, 8) == y, lax.rem(f, 2) == zr)
    for cond, full, sem in ((mine, vg, s_c), (listed, dr, s_d)):
        most = full.at[pl.ds(0, full.shape[0] - 1)]

        @pl.when(cond)
        def _():
            arrived(most, most, sem)

        @pl.when(jnp.logical_not(cond))
        def _():
            arrived(full, full, sem)

    arrived(dr, dr, r_d)
    sa = dr[0, 0]
    sb = dr[0, 1]
    for i in range(1, 16):
        sa = sa + dr[i, 0]
        sb = sb + dr[i, 1]
    inv_v = lax.rsqrt(sa[:, 64:128] + NORM_EPS)
    res_a = sa[:, 0:64] * lax.rsqrt(sb[:, 64:65] + NORM_EPS) * inv_v
    s2 = (sb[0:2] + sb[2:4]) + (sb[4:6] + sb[6:8])
    res_b = s2[:, 0:64] * lax.rsqrt(s2[:, 96:97] + NORM_EPS) * inv_v[0:2]
    pick = lax.rem(lax.div(f, 2), 4)
    for res, rows in ((res_a, pl.ds(0, 8)), (res_b, pl.ds(8, 2))):
        o = res[:, 0:16]
        for i in range(1, 4):
            o = jnp.where(pick == i, res[:, 16 * i : 16 * i + 16], o)
        out[rows, :] = o


def body(xt, ct, lt, xv, cv, lv, ad, au, mom1, mom2, rank_p, feat_p):
    dma = pltpu.SemaphoreType.DMA
    tile = lambda *lead: pltpu.VMEM(lead + (8, 128), F32)
    scratch = [
        pltpu.VMEM((2, NT + NV, HALF), BF16),
        pltpu.VMEM((2, 64, HALF), BF16),
        pltpu.VMEM((2, 16, 64), BF16),
        pltpu.VMEM((2, HALF, 256), BF16),
        pltpu.VMEM((2, 64, HALF), F32),
        pltpu.VMEM((2, 64, HALF), F32),
        pltpu.VMEM((10, SEG), jnp.int32),
        pltpu.VMEM((8, SEG), jnp.int32),
        tile(2, 8, 2),
        tile(8, 2),
        tile(7, 2),
        tile(2, 8, 2),
        tile(2, 8, 7),
        tile(8, 7),
        tile(7, 7),
        tile(2, 8, 7),
        pltpu.VMEM((16, 1024), F32),
        pltpu.VMEM((8, 1024), F32),
        pltpu.VMEM((2, 128, HALF), BF16),
        pltpu.VMEM((2, 32, 128), BF16),
        pltpu.VMEM((2, 640, HALF), BF16),
        tile(2, 8, 4),
        tile(8, 4),
        tile(7, 4),
        tile(2, 8, 5),
        tile(8, 5),
        tile(7, 5),
        tile(4),
        tile(5),
        tile(8, 4),
        tile(4, 5),
        tile(4, 2),
        tile(16, 2),
        dma((8,)),
        dma((2, 3)),
        dma((4,)), dma((4,)),
        dma, dma, dma, dma((4,)), dma, dma,
        dma, dma, dma, dma((4,)), dma, dma,
        dma, dma, dma, dma, dma, dma, dma, dma, dma, dma,
        pltpu.SemaphoreType.REGULAR((3,)),
    ]
    return pl.pallas_call(
        kernel,
        name="features",
        out_shape=pltpu.VMEM((10, 16), F32),
        in_specs=[pl.BlockSpec(memory_space=pltpu.HBM)] * 12,
        out_specs=pl.BlockSpec(memory_space=pltpu.VMEM),
        scratch_shapes=scratch,
        compiler_params=pltpu.CompilerParams(
            collective_id=0, has_side_effects=True, vmem_limit_bytes=60 << 20
        ),
    )(
        xt.reshape(NT, HALF), ct.reshape(NT, HALF), lt,
        xv.reshape(NV, HALF), cv.reshape(NV, HALF), lv,
        ad, au, mom1, mom2, jnp.swapaxes(rank_p, 1, 2), feat_p,
    )


def solution(mesh):
    placed = (
        P("dp", None, "fsdp"),
        P("dp", None, "fsdp"),
        P("dp", None),
        P("dp", None, "fsdp"),
        P("dp", None, "fsdp"),
        P("dp", None),
        P(None, "fsdp"),
        P(None, "fsdp"),
        P(None, None, "fsdp"),
        P(None, None, "fsdp"),
        P(),
        P(None, "fsdp", None),
    )
    return jax.shard_map(
        body, mesh=mesh, in_specs=placed, out_specs=P("dp", "fsdp"), check_vma=False
    )
```
